256 devices in a mesh: rows: 8 (over x, core), cols: 32 (over y, z).
Axes of the slice: x: 4, y: 4, z: 8, core: 2. Of those that a mesh axis runs over, the one named last changes fastest.
Arguments:
- blocks: bfloat16 [12288, 256, 256], P(('rows', 'cols')), may hold values from 0 to 0.0012969971
- block_row: int32 [12288], P(('rows', 'cols')), may hold values from 0 to 31
- block_col: int32 [12288], P(('rows', 'cols')), may hold values from 0 to 127
- block_count: int32 [256], P(('rows', 'cols')), may hold values from 12 to 48, as said below
- primal: float32 [1048576], P('cols'), may hold values from 0 to 1
- dual: float32 [65536], P('rows'), may hold values from 0 to 2
- cost: float32 [1048576], P('cols'), may hold values from 0.5 to 5
- demand: float32 [65536], P('rows'), may hold values from 0.05 to 5
- step: float32 [1], replicated, may hold values from 0.3 to 0.6
- fresh_pattern_blocks: bfloat16 [8192, 256, 256], P(('rows', 'cols')), may hold values from 0 to 0.0078125
- fresh_block_row: int32 [8192], P(('rows', 'cols')), may hold values from 0 to 255
- fresh_block_column: int32 [8192], P(('rows', 'cols')), may hold values from 0 to 31
- fresh_pattern_cost: float32 [2097152], P(('rows', 'cols')), may hold values from 0.5 to 5
Outputs:
- primal_out: float32 [1048576], P('cols')
- dual_out: float32 [65536], P('rows')
- reduced: float32 [2097152], P(('rows', 'cols'))
The draws below stay inside these ranges and needn't reach their ends.
Inputs may be any that keep to these rules, and one draw needn't show every extreme that they name: `block_count`: at least a quarter of the slots are live on every device, and some device has all 48 live.
All inputs are finite; a program needn't handle non-finite values.
Results may differ from the reference program's by a relative error of at most 0.0003.
Values sent between devices are 32-bit elements; how exact they have to be, the bound alone decides.
A program may use at most 64 MiB of HBM per device.

```python
import math
import jax
import jax.numpy as jnp
from jax import lax

BLOCK_EDGE = 256
ROW_BLOCK_COUNT = 32
CB_DEV = 128
SLOTS = 48
NEW_BLOCK_COUNT = 32
NEW_SLOT_COUNT = 32
ITERS = 2
NROW = 65536
NCOL = 1048576
NEWPAT = 2097152
N_ROWS = 8
N_COLS = 32


def draw_block_count(key, part):
    key = jax.random.fold_in(key, 1)
    first, second = jax.random.split(key)
    counts = jax.random.randint(first, (N_ROWS * N_COLS,), SLOTS // 4, SLOTS + 1)
    fullest = jax.random.randint(second, (), 0, N_ROWS * N_COLS)
    return jnp.where(jnp.arange(N_ROWS * N_COLS) == fullest, SLOTS, counts).astype(jnp.int32)


def plant(entries, own_key, low, high):
    index_at = [jax.random.randint(jax.random.fold_in(own_key, axis), (), 0, length) for axis, length in enumerate(entries.shape)]
    widest = entries.shape.index(max(entries.shape))
    neighbour = index_at[:widest] + [(index_at[widest] + 1) % entries.shape[widest]] + index_at[widest + 1:]
    return entries.at[tuple(index_at)].set(low).at[tuple(neighbour)].set(high)


def block_scale(own_key, dims, shards, least, top_value):
    level, own = 1.0, jax.random.fold_in(own_key, 6)
    for axis_at, blocks in shards:
        steps = jnp.exp(jax.random.uniform(jax.random.fold_in(own, axis_at), (blocks,), jnp.float32, least / len(shards), top_value / len(shards)))
        level = level * jnp.repeat(steps, dims[axis_at] // blocks).reshape([-1 if axis == axis_at else 1 for axis in range(len(dims))])
    return level


def setup_inputs(seed: int = 0) -> dict:
    key_list = jax.random.split(jax.random.key(seed), 14)
    blocks = jnp.clip(0.0012969971 * jax.random.uniform(key_list[0], (N_ROWS * N_COLS * SLOTS, BLOCK_EDGE, BLOCK_EDGE), jnp.float32) ** block_scale(key_list[0], (N_ROWS * N_COLS * SLOTS, BLOCK_EDGE, BLOCK_EDGE), ((0, 256),), -0.2, 0.2), 0.0, 0.0012969971).astype(jnp.bfloat16)
    block_row = plant(jax.random.randint(key_list[1], (N_ROWS * N_COLS * SLOTS,), 0, ROW_BLOCK_COUNT), jax.random.fold_in(key_list[1], 1), 0, ROW_BLOCK_COUNT - 1).astype(jnp.int32)
    block_col = plant(jax.random.randint(key_list[2], (N_ROWS * N_COLS * SLOTS,), 0, CB_DEV), jax.random.fold_in(key_list[2], 1), 0, CB_DEV - 1).astype(jnp.int32)
    block_count = draw_block_count(jax.random.fold_in(key_list[13], 71), 0)
    primal = jnp.clip(1.0 * jax.random.uniform(key_list[4], (NCOL,), jnp.float32) ** block_scale(key_list[4], (NCOL,), ((0, 32),), -0.2, 0.2), 0.0, 1.0)
    dual = jnp.clip(2.0 * jax.random.uniform(key_list[5], (NROW,), jnp.float32) ** block_scale(key_list[5], (NROW,), ((0, 8),), -0.2, 0.2), 0.0, 2.0)
    cost = jnp.clip(jnp.exp(math.log(5.0) - 2.3025851 * jax.random.uniform(key_list[6], (NCOL,), jnp.float32) ** block_scale(key_list[6], (NCOL,), ((0, 32),), -0.2, 0.2)), 0.5, 5.0)
    demand = jnp.clip(jnp.exp(math.log(5.0) - 4.6051702 * jax.random.uniform(key_list[7], (NROW,), jnp.float32) ** block_scale(key_list[7], (NROW,), ((0, 8),), -0.2, 0.2)), 0.05, 5.0)
    step = jnp.clip(jnp.exp(jax.random.uniform(key_list[8], (1,), jnp.float32, math.log(0.3), math.log(0.6))), 0.3, 0.6)
    fresh_pattern_blocks = jnp.clip(0.0078125 * jax.random.uniform(key_list[9], (N_ROWS * N_COLS * NEW_SLOT_COUNT, BLOCK_EDGE, BLOCK_EDGE), jnp.float32) ** block_scale(key_list[9], (N_ROWS * N_COLS * NEW_SLOT_COUNT, BLOCK_EDGE, BLOCK_EDGE), ((0, 256),), -0.2, 0.2), 0.0, 0.0078125).astype(jnp.bfloat16)
    fresh_block_row = plant(jax.random.randint(key_list[10], (N_ROWS * N_COLS * NEW_SLOT_COUNT,), 0, ROW_BLOCK_COUNT * N_ROWS), jax.random.fold_in(key_list[10], 1), 0, (ROW_BLOCK_COUNT * N_ROWS) - 1).astype(jnp.int32)
    fresh_block_column = plant(jax.random.randint(key_list[11], (N_ROWS * N_COLS * NEW_SLOT_COUNT,), 0, NEW_BLOCK_COUNT), jax.random.fold_in(key_list[11], 1), 0, NEW_BLOCK_COUNT - 1).astype(jnp.int32)
    fresh_pattern_cost = jnp.clip(jnp.exp(math.log(5.0) - 2.3025851 * jax.random.uniform(key_list[12], (NEWPAT,), jnp.float32) ** block_scale(key_list[12], (NEWPAT,), ((0, 256),), -0.2, 0.2)), 0.5, 5.0)
    return dict(blocks=blocks, block_row=block_row, block_col=block_col, block_count=block_count, primal=primal, dual=dual, cost=cost, demand=demand, step=step, fresh_pattern_blocks=fresh_pattern_blocks, fresh_block_row=fresh_block_row, fresh_block_column=fresh_block_column, fresh_pattern_cost=fresh_pattern_cost)


def multiply_blocks(blocks, grow, gcol, live, count_slots, vec, forward, nout):
    HI = lax.Precision.HIGHEST

    def visit(carry, dev):
        start = dev * count_slots
        blk = lax.dynamic_slice_in_dim(blocks, start, count_slots, 0).astype(jnp.float32)
        rows_i = lax.dynamic_slice_in_dim(grow, start, count_slots, 0)
        cols_i = lax.dynamic_slice_in_dim(gcol, start, count_slots, 0)
        alive = lax.dynamic_slice_in_dim(live, start, count_slots, 0)
        if forward:
            pieces = vec[cols_i]
            prod = jnp.einsum('sij,sj->si', blk, pieces, precision=HI) * alive[:, None]
            carry = carry.at[rows_i].add(prod)
        else:
            pieces = vec[rows_i]
            prod = jnp.einsum('sij,si->sj', blk, pieces, precision=HI) * alive[:, None]
            carry = carry.at[cols_i].add(prod)
        return (carry, None)
    start = jnp.zeros((nout, BLOCK_EDGE), jnp.float32)
    total, _ = lax.scan(visit, start, jnp.arange(N_ROWS * N_COLS, dtype=jnp.int32))
    return total.reshape(-1)

def reference(blocks, block_row, block_col, block_count, primal, dual, cost, demand, step, fresh_pattern_blocks, fresh_block_row, fresh_block_column, fresh_pattern_cost):
    row_block_number = ROW_BLOCK_COUNT * N_ROWS
    ncb = CB_DEV * N_COLS
    slot_ids = jnp.arange(N_ROWS * N_COLS * SLOTS, dtype=jnp.int32)
    owner = slot_ids // SLOTS
    grow = owner // N_COLS * ROW_BLOCK_COUNT + block_row
    gcol = owner % N_COLS * CB_DEV + block_col
    live = (slot_ids % SLOTS < block_count[owner]).astype(jnp.float32)
    omega = jnp.sqrt(jnp.sum(cost * cost)) / jnp.sqrt(jnp.sum(demand * demand))
    tau = step[0] / omega
    sigma = step[0] * omega
    current_primal, current_dual = (primal, dual)
    for turn in range(ITERS):
        back = multiply_blocks(blocks, grow, gcol, live, SLOTS, current_dual.reshape(row_block_number, BLOCK_EDGE), False, ncb)
        primal_next = jnp.maximum(0.0, current_primal - tau * (cost - back))
        extra = (2.0 * primal_next - current_primal).reshape(ncb, BLOCK_EDGE)
        fore = multiply_blocks(blocks, grow, gcol, live, SLOTS, extra, True, row_block_number)
        current_dual = jnp.maximum(0.0, current_dual + sigma * (demand - fore))
        current_primal = primal_next
    fresh_pattern_index = jnp.arange(N_ROWS * N_COLS * NEW_SLOT_COUNT, dtype=jnp.int32)
    fresh_global_column = fresh_pattern_index // NEW_SLOT_COUNT * NEW_BLOCK_COUNT + fresh_block_column
    unit_vector = jnp.ones((N_ROWS * N_COLS * NEW_SLOT_COUNT,), jnp.float32)
    reduced_costs = multiply_blocks(fresh_pattern_blocks, fresh_block_row, fresh_global_column, unit_vector, NEW_SLOT_COUNT, current_dual.reshape(row_block_number, BLOCK_EDGE), False, NEW_BLOCK_COUNT * N_ROWS * N_COLS)
    return (current_primal, current_dual, fresh_pattern_cost - reduced_costs)
```

```python
import jax
import jax.numpy as jnp
from jax import lax
from jax.sharding import PartitionSpec as P
from jax.experimental import pallas as pl
from jax.experimental.pallas import tpu as pltpu

MESH = pl.DeviceIdType.MESH
ITERS = 2
EDGE = 256
LANES = 128
SLOTS = 48
NEW = 32
XN, YN, ZN = 4, 4, 8
PLANE = YN * ZN
COLB = 128
ROWB = 32
CHUNK = 8
BF = jnp.bfloat16
F32 = jnp.float32
LOADS = 4


def split3(v):
    hi = v.astype(BF).astype(F32)
    rest = v - hi
    mid = rest.astype(BF).astype(F32)
    return hi, mid, rest - mid


def piece_tile(ref, at, lane_row):
    v = jnp.concatenate([ref[pl.ds(at, 1), :], ref[pl.ds(at + 1, 1), :]], axis=1)
    v = jnp.broadcast_to(v, (8, EDGE))
    hi, mid, lo = split3(v)
    tile = jnp.where(lane_row == 0, hi, jnp.where(lane_row == 1, mid, lo))
    return jnp.where(lane_row < 3, tile, 0.0).astype(BF)


def products(count, unroll, vec_ref, start_of, blk_ref, out_ref, transposed):
    lane_row = lax.broadcasted_iota(jnp.int32, (8, EDGE), 0)
    dims = (((1,), (1,)), ((), ())) if transposed else (((1,), (0,)), ((), ()))

    def step(i, _):
        for u in range(unroll):
            s = i * unroll + u
            tile = piece_tile(vec_ref, start_of(s), lane_row)
            res = lax.dot_general(tile, blk_ref[s], dims, preferred_element_type=F32)
            out_ref[pl.ds(s, 1), :] = jnp.sum(res, axis=0, keepdims=True)
        return 0

    lax.fori_loop(0, count // unroll, step, 0)


def scatter(hot, prod):
    out = None
    for part in split3(prod):
        term = jnp.dot(hot, part.astype(BF), preferred_element_type=F32)
        out = term if out is None else out + term
    return out


def put_pairs(ref, val, at=0):
    n = val.shape[0]
    ref[pl.ds(at, n, stride=2), :] = val[:, :LANES]
    ref[pl.ds(at + 1, n, stride=2), :] = val[:, LANES:]


def kernel(
    brow_s, bcol_s, cnt_s, frow_s, step_s,
    bcol_v, brow_v, fcol_v,
    primal, dual, cost, demand, fcost,
    blocks, fresh,
    primal_o, dual_o, reduced_o,
    blk, frs, prod, pbuf, meta, metabuf, dense, sib, costrow, costbuf,
    xbar, xcur, prodf, part, rsbuf, ybuf, yall, prodn, priced,
    load_sem, fresh_sem, px_send, px_recv, meta_send, meta_recv, cost_send, cost_recv,
    sib_send, sib_recv, rs_send, rs_recv, ag_send, ag_recv, fx_send, fx_recv, fs_send, fs_recv,
):
    r = lax.axis_index("rows")
    c = lax.axis_index("cols")
    x, core = r // 2, lax.rem(r, 2)
    y, z = c // ZN, lax.rem(c, ZN)
    per = SLOTS // LOADS

    def load(i):
        return pltpu.make_async_copy(
            blocks.at[pl.ds(i * per, per)], blk.at[pl.ds(i * per, per)], load_sem.at[i]
        )

    fresh_copy = pltpu.make_async_copy(fresh, frs, fresh_sem)
    for i in range(LOADS):
        load(i).start()

    def plane_peer(k):
        return lax.rem(y + k // ZN, YN), lax.rem(z + lax.rem(k, ZN), ZN)

    def x_peer(d):
        return (lax.rem(x + d, XN) * 2 + core, c)

    sibling = (x * 2 + 1 - core, c)

    barrier = pltpu.get_barrier_semaphore()

    def greet(k, _):
        ty, tz = plane_peer(k)
        pl.semaphore_signal(barrier, inc=1, device_id=(r, ty * ZN + tz), device_id_type=MESH)
        return 0

    def greet_x(d, _):
        pl.semaphore_signal(barrier, inc=1, device_id=x_peer(d), device_id_type=MESH)
        return 0

    lax.fori_loop(1, PLANE, greet, 0)
    lax.fori_loop(1, XN, greet_x, 0)
    pl.semaphore_signal(barrier, inc=1, device_id=sibling, device_id_type=MESH)

    lanes = lax.broadcasted_iota(jnp.int32, (1, SLOTS), 1)
    alive = lanes < cnt_s[0]
    my_cols = jnp.where(alive, bcol_v[...], -1)
    my_rows = jnp.where(alive, brow_v[...], -1)
    row_hot = (lax.broadcasted_iota(jnp.int32, (ROWB, SLOTS), 0) == my_rows).astype(F32).astype(BF)
    col_ids = lax.broadcasted_iota(jnp.int32, (COLB, SLOTS), 0).astype(F32)

    def col_hot(cols):
        return (col_ids == cols).astype(F32).astype(BF)

    dem_sq = jnp.sum(demand[...] * demand[...], axis=0, keepdims=True)
    meta[...] = jnp.zeros_like(meta)
    meta[0:1, 0:SLOTS] = my_cols.astype(F32)
    meta[1:2, :] = dem_sq
    costrow[...] = jnp.sum(cost[...] * cost[...], axis=0, keepdims=True)

    def back_products(vec_ref, out_ref):
        products(SLOTS, 12, vec_ref, lambda s: 2 * brow_s[s], blk, out_ref, False)

    for i in range(LOADS):
        load(i).wait()
    fresh_copy.start()

    back_products(dual, prod.at[0])
    pl.semaphore_wait(barrier, PLANE - 1 + XN - 1 + 1)

    my_chunk = lax.rem(y, 2) * 4 + lax.rem(z, 4)
    my_at = pl.multiple_of(my_chunk * CHUNK, CHUNK)
    tau = sigma = None
    for it in range(ITERS):
        def send_products(d, _, it=it):
            pltpu.make_async_remote_copy(
                src_ref=prod.at[it], dst_ref=pbuf.at[it, d - 1],
                send_sem=px_send.at[it], recv_sem=px_recv.at[it, d - 1],
                device_id=x_peer(d), device_id_type=MESH,
            ).start()
            return 0

        if it == 0:
            def send_meta(d, _):
                pltpu.make_async_remote_copy(
                    src_ref=meta, dst_ref=metabuf.at[d - 1],
                    send_sem=meta_send, recv_sem=meta_recv,
                    device_id=x_peer(d), device_id_type=MESH,
                ).start()
                return 0

            lax.fori_loop(1, XN, send_meta, 0)
        lax.fori_loop(1, XN, send_products, 0)
        if it == 0:
            def send_cost(k, _):
                ty, tz = plane_peer(k)
                pltpu.make_async_remote_copy(
                    src_ref=costrow, dst_ref=costbuf.at[k],
                    send_sem=cost_send, recv_sem=cost_recv,
                    device_id=(r, ty * ZN + tz), device_id_type=MESH,
                ).start()
                return 0

            lax.fori_loop(1, PLANE, send_cost, 0)
        total = scatter(col_hot(my_cols.astype(F32)), prod[it])
        if it == 0:
            pltpu.make_async_copy(metabuf, metabuf, meta_recv).wait()
        for d in range(XN - 1):
            pltpu.make_async_copy(pbuf.at[it, d], pbuf.at[it, d], px_recv.at[it, d]).wait()
            total = total + scatter(col_hot(metabuf[d, 0:1, 0:SLOTS]), pbuf[it, d])
        put_pairs(dense.at[it], total)
        if it == 0:
            dem4 = dem_sq + metabuf[0, 1:2, :] + metabuf[1, 1:2, :] + metabuf[2, 1:2, :]
            dense[it, 2 * COLB:, :] = jnp.broadcast_to(dem4, (8, LANES))
        to_sibling = pltpu.make_async_remote_copy(
            src_ref=dense.at[it], dst_ref=sib.at[it],
            send_sem=sib_send.at[it], recv_sem=sib_recv.at[it],
            device_id=sibling, device_id_type=MESH,
        )
        to_sibling.start()
        if it == 0:
            pltpu.make_async_copy(costbuf.at[pl.ds(1, PLANE - 1)], costbuf.at[pl.ds(1, PLANE - 1)], cost_recv).wait()
            costbuf[0] = costrow[...]
            cost_total = jnp.sum(jnp.sum(costbuf[...], axis=0), axis=1, keepdims=True)
        to_sibling.wait_recv()
        if it == 0:
            dem_total = jnp.sum(dem4 + sib[it, 2 * COLB:2 * COLB + 1, :], axis=1, keepdims=True)
            omega = jnp.sqrt(cost_total) / jnp.sqrt(dem_total)
            tau = step_s[0] / omega
            sigma = step_s[0] * omega
        was = primal[...] if it == 0 else xcur[...]
        back = dense[it, 0:2 * COLB, :] + sib[it, 0:2 * COLB, :]
        now = jnp.maximum(0.0, was - tau * (cost[...] - back))
        xbar[...] = 2.0 * now - was
        if it == ITERS - 1:
            primal_o[...] = now
        else:
            xcur[...] = now

        products(SLOTS, 12, xbar, lambda s: 2 * bcol_s[s], blk, prodf, True)
        put_pairs(part.at[it], scatter(row_hot, prodf[...]))

        def send_chunk(k, _, it=it):
            ty, tz = plane_peer(k)
            at = pl.multiple_of((lax.rem(ty, 2) * 4 + lax.rem(tz, 4)) * CHUNK, CHUNK)
            pltpu.make_async_remote_copy(
                src_ref=part.at[it, pl.ds(at, CHUNK)], dst_ref=rsbuf.at[it, k],
                send_sem=rs_send.at[it], recv_sem=rs_recv.at[it],
                device_id=(r, ty * ZN + tz), device_id_type=MESH,
            ).start()
            return 0

        lax.fori_loop(1, PLANE, send_chunk, 0)
        mine = part[it, pl.ds(my_at, CHUNK), :]
        rs_all = rsbuf.at[it, pl.ds(1, PLANE - 1)]
        pltpu.make_async_copy(rs_all, rs_all, rs_recv.at[it]).wait()
        fore = mine + jnp.sum(rsbuf[it, 1:PLANE], axis=0)
        y_was = dual[pl.ds(my_at, CHUNK), :] if it == 0 else ybuf[it - 1, pl.ds(my_at, CHUNK), :]
        y_now = jnp.maximum(0.0, y_was + sigma * (demand[pl.ds(my_at, CHUNK), :] - fore))
        held = ybuf.at[it] if it < ITERS - 1 else yall.at[core, x]
        held[pl.ds(my_at, CHUNK), :] = y_now

        def send_dual(k, _, it=it, held=held):
            ty = lax.rem(y + k // 4, YN)
            tz = lax.rem(z + lax.rem(k, 4) + ZN - 1, ZN)
            pltpu.make_async_remote_copy(
                src_ref=held.at[pl.ds(my_at, CHUNK)], dst_ref=held.at[pl.ds(my_at, CHUNK)],
                send_sem=ag_send.at[it], recv_sem=ag_recv.at[it],
                device_id=(r, ty * ZN + tz), device_id_type=MESH,
            ).start()
            return 0

        send_dual(0, 0)
        lax.fori_loop(2, 8, send_dual, 0)
        seven = held.at[pl.ds(0, 7 * CHUNK)]
        pltpu.make_async_copy(seven, seven, ag_recv.at[it]).wait()
        if it < ITERS - 1:
            back_products(ybuf.at[it], prod.at[it + 1])

    own = yall.at[core, x]

    def send_rows(d, _):
        pltpu.make_async_remote_copy(
            src_ref=own, dst_ref=own,
            send_sem=fx_send, recv_sem=fx_recv,
            device_id=x_peer(d), device_id_type=MESH,
        ).start()
        return 0

    lax.fori_loop(1, XN, send_rows, 0)
    dual_o[...] = own[...]
    fresh_copy.wait()
    three = yall.at[core, pl.ds(0, XN - 1)]
    pltpu.make_async_copy(three, three, fx_recv).wait()
    half = pltpu.make_async_remote_copy(
        src_ref=yall.at[core], dst_ref=yall.at[core],
        send_sem=fs_send, recv_sem=fs_recv,
        device_id=sibling, device_id_type=MESH,
    )
    half.start()
    half.wait_recv()

    yflat = yall.reshape(2 * XN * 2 * ROWB, LANES)

    def new_at(s):
        block = frow_s[s]
        rr = block // ROWB
        return lax.rem(rr, 2) * (XN * 2 * ROWB) + (rr // 2) * (2 * ROWB) + lax.rem(block, ROWB) * 2

    products(NEW, 8, yflat, new_at, frs, prodn, False)
    new_hot = (lax.broadcasted_iota(jnp.int32, (NEW, NEW), 0) == fcol_v[...]).astype(F32).astype(BF)
    put_pairs(priced, scatter(new_hot, prodn[...]))
    reduced_o[...] = fcost[...] - priced[...]

    half.wait_send()
    pltpu.make_async_copy(three, three, fx_send).wait()
    meta3 = metabuf
    pltpu.make_async_copy(meta3, meta3, meta_send).wait()
    cost31 = costbuf.at[pl.ds(1, PLANE - 1)]
    pltpu.make_async_copy(cost31, cost31, cost_send).wait()
    for it in range(ITERS):
        pltpu.make_async_copy(pbuf.at[it], pbuf.at[it], px_send.at[it]).wait()
        pltpu.make_async_copy(sib.at[it], sib.at[it], sib_send.at[it]).wait()
        rs_all = rsbuf.at[it, pl.ds(1, PLANE - 1)]
        pltpu.make_async_copy(rs_all, rs_all, rs_send.at[it]).wait()
        seven = ybuf.at[it, pl.ds(0, 7 * CHUNK)]
        pltpu.make_async_copy(seven, seven, ag_send.at[it]).wait()


def local(
    blocks, block_row, block_col, block_count, primal, dual, cost, demand, step,
    fresh_pattern_blocks, fresh_block_row, fresh_block_column, fresh_pattern_cost,
):
    smem = pl.BlockSpec(memory_space=pltpu.SMEM)
    vmem = pl.BlockSpec(memory_space=pltpu.VMEM)
    hbm = pl.BlockSpec(memory_space=pl.ANY)
    dma = pltpu.SemaphoreType.DMA
    rows2 = lambda v: v.reshape(-1, LANES)
    outs = pl.pallas_call(
        kernel,
        out_shape=(
            jax.ShapeDtypeStruct((2 * COLB, LANES), F32),
            jax.ShapeDtypeStruct((2 * ROWB, LANES), F32),
            jax.ShapeDtypeStruct((2 * NEW, LANES), F32),
        ),
        in_specs=[smem] * 5 + [vmem] * 8 + [hbm] * 2,
        out_specs=(vmem, vmem, vmem),
        scratch_shapes=[
            pltpu.VMEM((SLOTS, EDGE, EDGE), BF),
            pltpu.VMEM((NEW, EDGE, EDGE), BF),
            pltpu.VMEM((ITERS, SLOTS, EDGE), F32),
            pltpu.VMEM((ITERS, XN - 1, SLOTS, EDGE), F32),
            pltpu.VMEM((8, LANES), F32),
            pltpu.VMEM((XN - 1, 8, LANES), F32),
            pltpu.VMEM((ITERS, 2 * COLB + 8, LANES), F32),
            pltpu.VMEM((ITERS, 2 * COLB + 8, LANES), F32),
            pltpu.VMEM((1, LANES), F32),
            pltpu.VMEM((PLANE, 1, LANES), F32),
            pltpu.VMEM((2 * COLB, LANES), F32),
            pltpu.VMEM((2 * COLB, LANES), F32),
            pltpu.VMEM((SLOTS, EDGE), F32),
            pltpu.VMEM((ITERS, 2 * ROWB, LANES), F32),
            pltpu.VMEM((ITERS, PLANE, CHUNK, LANES), F32),
            pltpu.VMEM((ITERS, 2 * ROWB, LANES), F32),
            pltpu.VMEM((2, XN, 2 * ROWB, LANES), F32),
            pltpu.VMEM((NEW, EDGE), F32),
            pltpu.VMEM((2 * NEW, LANES), F32),
            dma((LOADS,)), dma,
            dma((ITERS,)), dma((ITERS, XN - 1)), dma, dma, dma, dma,
            dma((ITERS,)), dma((ITERS,)), dma((ITERS,)), dma((ITERS,)),
            dma((ITERS,)), dma((ITERS,)), dma, dma, dma, dma,
        ],
        compiler_params=pltpu.CompilerParams(
            collective_id=0, has_side_effects=True, vmem_limit_bytes=40 * 2**20
        ),
    )(
        block_row, block_col, block_count, fresh_block_row, step,
        block_col.reshape(1, -1), block_row.reshape(1, -1), fresh_block_column.reshape(1, -1),
        rows2(primal), rows2(dual), rows2(cost), rows2(demand), rows2(fresh_pattern_cost),
        blocks, fresh_pattern_blocks,
    )
    return tuple(o.reshape(-1) for o in outs)


def solution(mesh):
    both = ("rows", "cols")
    placed = (
        P(both, None, None), P(both), P(both), P(both),
        P("cols"), P("rows"), P("cols"), P("rows"), P(),
        P(both, None, None), P(both), P(both), P(both),
    )
    return jax.shard_map(
        local, mesh=mesh, in_specs=placed,
        out_specs=(P("cols"), P("rows"), P(both)), check_vma=False,
    )
```

```python
import jax
import jax.numpy as jnp
from jax import lax
from jax.sharding import PartitionSpec as P
from jax.experimental import pallas as pl
from jax.experimental.pallas import tpu as pltpu

MESH = pl.DeviceIdType.MESH
ITERS = 2
EDGE = 256
LANES = 128
SLOTS = 48
NEW = 32
XN, YN, ZN = 4, 4, 8
PLANE = YN * ZN
COLB = 128
ROWB = 32
CHUNK = 8
BF = jnp.bfloat16
F32 = jnp.float32
LOADS = 4
UNROLL = 12
UNROLL_NEW = 8


def split3(v):
    hi = v.astype(BF).astype(F32)
    rest = v - hi
    mid = rest.astype(BF).astype(F32)
    return hi, mid, rest - mid


def piece_tile(ref, at, lane_row):
    v = jnp.concatenate([ref[pl.ds(at, 1), :], ref[pl.ds(at + 1, 1), :]], axis=1)
    v = jnp.broadcast_to(v, (8, EDGE))
    hi, mid, lo = split3(v)
    tile = jnp.where(lane_row == 0, hi, jnp.where(lane_row == 1, mid, lo))
    return jnp.where(lane_row < 3, tile, 0.0).astype(BF)


def products(count, unroll, vec_ref, start_of, blk_ref, out_ref, transposed):
    lane_row = lax.broadcasted_iota(jnp.int32, (8, EDGE), 0)
    dims = (((1,), (1,)), ((), ())) if transposed else (((1,), (0,)), ((), ()))

    def step(i, _):
        for u in range(unroll):
            s = i * unroll + u
            tile = piece_tile(vec_ref, start_of(s), lane_row)
            res = lax.dot_general(tile, blk_ref[s], dims, preferred_element_type=F32)
            out_ref[pl.ds(s, 1), :] = jnp.sum(res, axis=0, keepdims=True)
        return 0

    lax.fori_loop(0, count // unroll, step, 0)


def scatter(hot, prod):
    out = None
    for part in split3(prod):
        term = jnp.dot(hot, part.astype(BF), preferred_element_type=F32)
        out = term if out is None else out + term
    return out


def put_pairs(ref, val, at=0):
    n = val.shape[0]
    ref[pl.ds(at, n, stride=2), :] = val[:, :LANES]
    ref[pl.ds(at + 1, n, stride=2), :] = val[:, LANES:]


def send(src, dst, send_sem, recv_sem, device):
    pltpu.make_async_remote_copy(
        src_ref=src, dst_ref=dst, send_sem=send_sem, recv_sem=recv_sem,
        device_id=device, device_id_type=MESH,
    ).start()


def wait_for(ref, sem):
    pltpu.make_async_copy(ref, ref, sem).wait()


def fetch(src, dst, sem):
    copy = pltpu.make_async_copy(src, dst, sem)
    copy.start()
    return copy


def kernel(
    brow_h, bcol_h, cnt_h, frow_h, step_h, bcolv_h, browv_h, fcolv_h,
    primal_h, dual_h, cost_h, demand_h, fcost_h, blocks, fresh,
    primal_oh, dual_oh, reduced_oh,
    primal_o, dual_o, reduced_o, out_sem,
    brow_s, bcol_s, cnt_s, frow_s, step_s, bcol_v, brow_v, fcol_v,
    primal, dual, cost, demand, fcost,
    blk, frs, prod, pbuf, meta, metabuf, dense, sib, costrow, costbuf,
    xbar, xcur, prodf, part, rsbuf, ybuf, yall, prodn, priced,
    in_sem, load_sem, fresh_sem, px_send, px_recv, meta_send, meta_recv, cost_send, cost_recv,
    sib_send, sib_recv, rs_send, rs_recv, ag_send, ag_recv, fs_send, fs_recv,
):
    r = lax.axis_index("rows")
    c = lax.axis_index("cols")
    x, core = r // 2, lax.rem(r, 2)
    y, z = c // ZN, lax.rem(c, ZN)
    per = SLOTS // LOADS

    first = [
        fetch(src, dst, in_sem.at[i])
        for i, (src, dst) in enumerate([(brow_h, brow_s), (dual_h, dual)])
    ]
    loads = [
        fetch(blocks.at[pl.ds(i * per, per)], blk.at[pl.ds(i * per, per)], load_sem.at[i])
        for i in range(LOADS)
    ]
    pairs = [
        (cnt_h, cnt_s), (bcolv_h, bcol_v), (browv_h, brow_v), (cost_h, cost), (demand_h, demand),
        (step_h, step_s), (bcol_h, bcol_s), (primal_h, primal),
        (frow_h, frow_s), (fcolv_h, fcol_v), (fcost_h, fcost),
    ]
    rest = [fetch(src, dst, in_sem.at[i + 2]) for i, (src, dst) in enumerate(pairs)]

    def plane_peer(j):
        return lax.rem(y + 2 + j // ZN, YN), lax.rem(z + 4 + lax.rem(j, ZN), ZN)

    def x_peer(d):
        return (lax.rem(x + d, XN) * 2 + core, c)

    def each_plane(do):
        lax.fori_loop(0, 20, lambda j, _: (do(j), 0)[1], 0)
        lax.fori_loop(21, PLANE, lambda j, _: (do(j), 0)[1], 0)

    sibling = (x * 2 + 1 - core, c)
    barrier = pltpu.get_barrier_semaphore()

    def greet(device):
        pl.semaphore_signal(barrier, inc=1, device_id=device, device_id_type=MESH)

    def greet_plane(j):
        ty, tz = plane_peer(j)
        greet((r, ty * ZN + tz))

    each_plane(greet_plane)
    lax.fori_loop(1, XN, lambda d, _: (greet(x_peer(d)), 0)[1], 0)
    greet(sibling)

    def back_products(vec_ref, out_ref):
        products(SLOTS, UNROLL, vec_ref, lambda s: 2 * brow_s[s], blk, out_ref, False)

    for copy in first + loads:
        copy.wait()
    fresh_copy = fetch(fresh, frs, fresh_sem)
    back_products(dual, prod.at[0])

    for copy in rest:
        copy.wait()
    lanes = lax.broadcasted_iota(jnp.int32, (1, SLOTS), 1)
    alive = lanes < cnt_s[0]
    my_cols = jnp.where(alive, bcol_v[...], -1)
    my_rows = jnp.where(alive, brow_v[...], -1)
    row_hot = (lax.broadcasted_iota(jnp.int32, (ROWB, SLOTS), 0) == my_rows).astype(F32).astype(BF)
    col_ids = lax.broadcasted_iota(jnp.int32, (COLB, SLOTS), 0).astype(F32)

    def col_hot(cols):
        return (col_ids == cols).astype(F32).astype(BF)

    dem_sq = jnp.sum(demand[...] * demand[...], axis=0, keepdims=True)
    meta[...] = jnp.zeros_like(meta)
    meta[0:1, 0:SLOTS] = my_cols.astype(F32)
    meta[1:2, :] = dem_sq
    costrow[...] = jnp.sum(cost[...] * cost[...], axis=0, keepdims=True)

    pl.semaphore_wait(barrier, PLANE - 1 + XN - 1 + 1)

    my_chunk = lax.rem(y, 2) * 4 + lax.rem(z, 4)
    my_at = pl.multiple_of(my_chunk * CHUNK, CHUNK)
    tau = sigma = None
    for it in range(ITERS):
        def send_products(d, _, it=it):
            if it == 0:
                send(meta, metabuf.at[d - 1], meta_send, meta_recv, x_peer(d))
            send(prod.at[it], pbuf.at[it, d - 1], px_send.at[it], px_recv.at[it, d - 1], x_peer(d))
            return 0

        lax.fori_loop(1, XN, send_products, 0)
        if it == 0:
            def send_cost(j):
                ty, tz = plane_peer(j)
                send(costrow, costbuf.at[j], cost_send, cost_recv, (r, ty * ZN + tz))

            each_plane(send_cost)
        total = scatter(col_hot(my_cols.astype(F32)), prod[it])
        if it == 0:
            wait_for(metabuf, meta_recv)
        for d in (0, 2, 1):
            wait_for(pbuf.at[it, d], px_recv.at[it, d])
            total = total + scatter(col_hot(metabuf[d, 0:1, 0:SLOTS]), pbuf[it, d])
        put_pairs(dense.at[it], total)
        if it == 0:
            dem4 = dem_sq + metabuf[0, 1:2, :] + metabuf[1, 1:2, :] + metabuf[2, 1:2, :]
            dense[it, 2 * COLB:, :] = jnp.broadcast_to(dem4, (8, LANES))
        send(dense.at[it], sib.at[it], sib_send.at[it], sib_recv.at[it], sibling)
        if it == 0:
            wait_for(costbuf.at[pl.ds(0, PLANE - 1)], cost_recv)
            costbuf[20] = costrow[...]
            cost_total = jnp.sum(jnp.sum(costbuf[...], axis=0), axis=1, keepdims=True)
        wait_for(sib.at[it], sib_recv.at[it])
        if it == 0:
            dem_total = jnp.sum(dem4 + sib[it, 2 * COLB:2 * COLB + 1, :], axis=1, keepdims=True)
            omega = jnp.sqrt(cost_total) / jnp.sqrt(dem_total)
            tau = step_s[0] / omega
            sigma = step_s[0] * omega
        was = primal[...] if it == 0 else xcur[...]
        back = dense[it, 0:2 * COLB, :] + sib[it, 0:2 * COLB, :]
        now = jnp.maximum(0.0, was - tau * (cost[...] - back))
        xbar[...] = 2.0 * now - was
        if it == ITERS - 1:
            primal_o[...] = now
            put_primal = fetch(primal_o, primal_oh, out_sem.at[0])
        else:
            xcur[...] = now

        products(SLOTS, UNROLL, xbar, lambda s: 2 * bcol_s[s], blk, prodf, True)
        put_pairs(part.at[it], scatter(row_hot, prodf[...]))

        def send_chunk(j, it=it):
            ty, tz = plane_peer(j)
            at = pl.multiple_of((lax.rem(ty, 2) * 4 + lax.rem(tz, 4)) * CHUNK, CHUNK)
            send(part.at[it, pl.ds(at, CHUNK)], rsbuf.at[it, j], rs_send.at[it], rs_recv.at[it],
                 (r, ty * ZN + tz))

        each_plane(send_chunk)
        rsbuf[it, 20] = part[it, pl.ds(my_at, CHUNK), :]
        wait_for(rsbuf.at[it, pl.ds(0, PLANE - 1)], rs_recv.at[it])
        fore = jnp.sum(rsbuf[it], axis=0)
        y_was = dual[pl.ds(my_at, CHUNK), :] if it == 0 else ybuf[it - 1, pl.ds(my_at, CHUNK), :]
        y_now = jnp.maximum(0.0, y_was + sigma * (demand[pl.ds(my_at, CHUNK), :] - fore))
        held = ybuf.at[it] if it < ITERS - 1 else yall.at[core, x]
        held[pl.ds(my_at, CHUNK), :] = y_now
        chunk = held.at[pl.ds(my_at, CHUNK)]

        def send_dual(dx, k, it=it, chunk=chunk):
            ty = lax.rem(y + k // 4, YN)
            tz = lax.rem(z + lax.rem(k, 4) + ZN - 1, ZN)
            send(chunk, chunk, ag_send.at[it], ag_recv.at[it],
                 (lax.rem(x + dx, XN) * 2 + core, ty * ZN + tz))
            return 0

        if it == ITERS - 1:
            lax.fori_loop(0, 3 * 8, lambda m, _: send_dual(lax.rem(m // 8 + 1, 3) + 1, lax.rem(m, 8)), 0)
        lax.fori_loop(2, 8, lambda k, _: send_dual(0, k), 0)
        send_dual(0, 0)
        if it < ITERS - 1:
            wait_for(held.at[pl.ds(0, 7 * CHUNK)], ag_recv.at[it])
            back_products(held, prod.at[it + 1])

    new_hot = (lax.broadcasted_iota(jnp.int32, (NEW, NEW), 0) == fcol_v[...]).astype(F32).astype(BF)
    fresh_copy.wait()
    wait_for(rsbuf.at[0, pl.ds(0, PLANE - 1)], ag_recv.at[ITERS - 1])
    send(yall.at[core], yall.at[core], fs_send, fs_recv, sibling)
    dual_o[...] = yall[core, x]
    put_dual = fetch(dual_o, dual_oh, out_sem.at[1])
    wait_for(yall.at[core], fs_recv)

    yflat = yall.reshape(2 * XN * 2 * ROWB, LANES)

    def new_at(s):
        block = frow_s[s]
        rr = block // ROWB
        return lax.rem(rr, 2) * (XN * 2 * ROWB) + (rr // 2) * (2 * ROWB) + lax.rem(block, ROWB) * 2

    products(NEW, UNROLL_NEW, yflat, new_at, frs, prodn, False)
    put_pairs(priced, scatter(new_hot, prodn[...]))
    reduced_o[...] = fcost[...] - priced[...]
    put_reduced = fetch(reduced_o, reduced_oh, out_sem.at[2])

    put_primal.wait()
    put_dual.wait()
    put_reduced.wait()
    wait_for(yall.at[core], fs_send)
    wait_for(metabuf, meta_send)
    wait_for(costbuf.at[pl.ds(0, PLANE - 1)], cost_send)
    for it in range(ITERS):
        wait_for(pbuf.at[it], px_send.at[it])
        wait_for(sib.at[it], sib_send.at[it])
        wait_for(rsbuf.at[it, pl.ds(0, PLANE - 1)], rs_send.at[it])
        wait_for(rsbuf.at[it, pl.ds(0, 7 if it < ITERS - 1 else PLANE - 1)], ag_send.at[it])


def local(
    blocks, block_row, block_col, block_count, primal, dual, cost, demand, step,
    fresh_pattern_blocks, fresh_block_row, fresh_block_column, fresh_pattern_cost,
):
    hbm = pl.BlockSpec(memory_space=pltpu.HBM)
    dma = pltpu.SemaphoreType.DMA
    smem_i = lambda n: pltpu.SMEM((n,), jnp.int32)
    vec_i = lambda n: pltpu.VMEM((1, n), jnp.int32)
    f32 = lambda *shape: pltpu.VMEM(shape, F32)
    rows2 = lambda v: v.reshape(-1, LANES)
    outs = pl.pallas_call(
        kernel,
        out_shape=(
            jax.ShapeDtypeStruct((2 * COLB, LANES), F32),
            jax.ShapeDtypeStruct((2 * ROWB, LANES), F32),
            jax.ShapeDtypeStruct((2 * NEW, LANES), F32),
        ),
        in_specs=[hbm] * 15,
        out_specs=(hbm, hbm, hbm),
        scratch_shapes=[
            f32(2 * COLB, LANES), f32(2 * ROWB, LANES), f32(2 * NEW, LANES), dma((3,)),
            smem_i(SLOTS), smem_i(SLOTS), smem_i(1), smem_i(NEW), pltpu.SMEM((1,), F32),
            vec_i(SLOTS), vec_i(SLOTS), vec_i(NEW),
            f32(2 * COLB, LANES), f32(2 * ROWB, LANES), f32(2 * COLB, LANES), f32(2 * ROWB, LANES),
            f32(2 * NEW, LANES),
            pltpu.VMEM((SLOTS, EDGE, EDGE), BF),
            pltpu.VMEM((NEW, EDGE, EDGE), BF),
            f32(ITERS, SLOTS, EDGE), f32(ITERS, XN - 1, SLOTS, EDGE),
            f32(8, LANES), f32(XN - 1, 8, LANES),
            f32(ITERS, 2 * COLB + 8, LANES), f32(ITERS, 2 * COLB + 8, LANES),
            f32(1, LANES), f32(PLANE, 1, LANES),
            f32(2 * COLB, LANES), f32(2 * COLB, LANES), f32(SLOTS, EDGE),
            f32(ITERS, 2 * ROWB, LANES), f32(ITERS, PLANE, CHUNK, LANES),
            f32(ITERS, 2 * ROWB, LANES), f32(2, XN, 2 * ROWB, LANES),
            f32(NEW, EDGE), f32(2 * NEW, LANES),
            dma((13,)), dma((LOADS,)), dma,
            dma((ITERS,)), dma((ITERS, XN - 1)), dma, dma, dma, dma,
            dma((ITERS,)), dma((ITERS,)), dma((ITERS,)), dma((ITERS,)),
            dma((ITERS,)), dma((ITERS,)), dma, dma,
        ],
        compiler_params=pltpu.CompilerParams(
            collective_id=0, has_side_effects=True, vmem_limit_bytes=60 * 2**20
        ),
    )(
        block_row, block_col, block_count, fresh_block_row, step,
        block_col.reshape(1, -1), block_row.reshape(1, -1), fresh_block_column.reshape(1, -1),
        rows2(primal), rows2(dual), rows2(cost), rows2(demand), rows2(fresh_pattern_cost),
        blocks, fresh_pattern_blocks,
    )
    def hand_over(*refs):
        sems = refs[-1]
        ins = [fetch(refs[i], refs[i + 6], sems.at[i]) for i in range(3)]
        copies = []
        for i in (0, 1, 2):
            ins[i].wait()
            copies.append(fetch(refs[i + 6], refs[i + 3], sems.at[i + 3]))
        for copy in copies:
            copy.wait()

    outs = pl.pallas_call(
        hand_over,
        out_shape=tuple(jax.ShapeDtypeStruct(o.shape, F32) for o in outs),
        in_specs=[hbm] * 3,
        out_specs=(hbm, hbm, hbm),
        scratch_shapes=[pltpu.VMEM(o.shape, F32) for o in outs] + [dma((6,))],
        compiler_params=pltpu.CompilerParams(vmem_limit_bytes=60 * 2**20),
    )(*outs)
    return tuple(o.reshape(-1) for o in outs)


def solution(mesh):
    both = ("rows", "cols")
    placed = (
        P(both, None, None), P(both), P(both), P(both),
        P("cols"), P("rows"), P("cols"), P("rows"), P(),
        P(both, None, None), P(both), P(both), P(both),
    )
    return jax.shard_map(
        local, mesh=mesh, in_specs=placed,
        out_specs=(P("cols"), P("rows"), P(both)), check_vma=False,
    )
```

```python
import jax
import jax.numpy as jnp
from jax import lax
from jax.sharding import PartitionSpec as P
from jax.experimental import pallas as pl
from jax.experimental.pallas import tpu as pltpu

MESH = pl.DeviceIdType.MESH
ITERS = 2
EDGE = 256
LANES = 128
SLOTS = 48
HALF = SLOTS // 2
NEW = 32
XN, YN, ZN = 4, 4, 8
PLANE = YN * ZN
COLB = 128
ROWB = 32
CHUNK = 8
PAD = 64
BF = jnp.bfloat16
F32 = jnp.float32
LOADS = 4
UNROLL = 24
UNROLL_NEW = 16
UNROLL_T = 4


def hops(p):
    ring = lambda d, n: min(d % n, -d % n)
    return ring(p[0], XN) + ring(p[1], YN) + ring(p[2], ZN)


def far_first(peers):
    return sorted([p for p in peers if hops(p)], key=lambda p: -hops(p))


PLANE_PEERS = far_first([(0, dy, dz) for dy in range(YN) for dz in range(ZN)])
NEAR = [(0, dy, dz) for dy in (0, 1) for dz in (-1, 0, 1, 2)]
NEAR_PEERS = far_first(NEAR)
LAST_PEERS = far_first([(dx, dy, dz) for dx in range(XN) for _, dy, dz in NEAR])
X_PEERS = (2, 1, 3)


def split3(v):
    hi = v.astype(BF).astype(F32)
    rest = v - hi
    mid = rest.astype(BF).astype(F32)
    return hi, mid, rest - mid


def piece_tile(ref, at, lane_row):
    v = jnp.concatenate([ref[pl.ds(at, 1), :], ref[pl.ds(at + 1, 1), :]], axis=1)
    v = jnp.broadcast_to(v, (8, EDGE))
    hi, mid, lo = split3(v)
    tile = jnp.where(lane_row == 0, hi, jnp.where(lane_row == 1, mid, lo))
    return jnp.where(lane_row < 3, tile, 0.0).astype(BF)


def put_tiles(ref, val):
    n = val.shape[0]
    for k, part in enumerate(split3(val)):
        for h in range(2):
            ref[h, pl.ds(k, n, stride=8), :] = part[:, h * LANES:(h + 1) * LANES]


def pairs(ref, n):
    return jnp.concatenate([ref[pl.ds(0, n, stride=2), :], ref[pl.ds(1, n, stride=2), :]], axis=1)


def put_pairs(ref, val):
    n = val.shape[0]
    ref[pl.ds(0, n, stride=2), :] = val[:, :LANES]
    ref[pl.ds(1, n, stride=2), :] = val[:, LANES:]


def products(first, count, unroll, tile_of, blk_ref, out_ref):
    def step(i, _):
        for u in range(unroll):
            s = first + i * unroll + u
            res = jnp.dot(tile_of(s), blk_ref[s], preferred_element_type=F32)
            for h in range(2):
                out_ref[h, pl.ds(pl.multiple_of(s * 8, 8), 8), :] = res[:, h * LANES:(h + 1) * LANES]
        return 0

    if count == unroll:
        step(0, 0)
    else:
        lax.fori_loop(0, count // unroll, step, 0)


def summed(ref, first, count):
    def half(h):
        parts = [ref[h, pl.ds(first * 8 + k, count, stride=8), :] for k in range(3)]
        return parts[0] + parts[1] + parts[2]

    return jnp.concatenate([half(0), half(1)], axis=1)


def hot3(ids, row):
    lane = lax.broadcasted_iota(jnp.int32, (1, LANES), 1)
    third = jnp.where(lane < PAD, row, -1.0)
    n = ids.shape[0]
    hot = [(ids == jnp.broadcast_to(v, (n, LANES))).astype(F32).astype(BF) for v in (row, third)]
    return jnp.concatenate(hot, axis=1)


def scatter(hot, prod):
    n = prod.shape[0]
    zeros = jnp.zeros((PAD - n, EDGE), BF)
    rows = []
    for part in split3(prod):
        rows += [part.astype(BF), zeros]
    rows.append(jnp.zeros((PAD, EDGE), BF))
    return jnp.dot(hot, jnp.concatenate(rows, axis=0), preferred_element_type=F32)


def send(src, dst, send_sem, recv_sem, device):
    pltpu.make_async_remote_copy(
        src_ref=src, dst_ref=dst, send_sem=send_sem, recv_sem=recv_sem,
        device_id=device, device_id_type=MESH,
    ).start()


def wait_for(ref, sem):
    pltpu.make_async_copy(ref, ref, sem).wait()


def fetch(src, dst, sem):
    copy = pltpu.make_async_copy(src, dst, sem)
    copy.start()
    return copy


def kernel(
    brow_h, bcol_h, cnt_h, frow_h, step_h, bcolv_h, browv_h, fcolv_h,
    primal_h, dual_h, cost_h, demand_h, fcost_h, blocks, fresh,
    primal_oh, dual_oh, reduced_oh,
    primal_o, dual_o, reduced_o, out_sem,
    brow_s, bcol_s, cnt_s, frow_s, step_s, bcol_v, brow_v, fcol_v,
    primal, dual, cost, demand, fcost, rows,
    blk, blk_t, frs, prod, pbuf, meta, metabuf, dense, sib, demrow, costrow, costbuf,
    xcur, price, xtile, ytile, prod8, part, rsbuf, ybuf, yall, priced,
    in_sem, load_sem, fresh_sem, px_send, px_recv, meta_send, meta_recv, cost_send, cost_recv,
    dem_send, dem_recv, sib_send, sib_recv, rs_send, rs_recv, ag_send, ag_recv, fs_send, fs_recv,
):
    r = lax.axis_index("rows")
    c = lax.axis_index("cols")
    x, core = r // 2, lax.rem(r, 2)
    y, z = c // ZN, lax.rem(c, ZN)
    per = SLOTS // LOADS

    first = [
        fetch(src, dst, in_sem.at[i])
        for i, (src, dst) in enumerate([(brow_h, brow_s), (dual_h, dual)])
    ]
    loads = [
        fetch(blocks.at[pl.ds(i * per, per)], blk.at[pl.ds(i * per, per)], load_sem.at[i])
        for i in range(LOADS)
    ]
    inputs = [
        (cnt_h, cnt_s), (bcolv_h, bcol_v), (browv_h, brow_v), (cost_h, cost), (demand_h, demand),
        (step_h, step_s), (bcol_h, bcol_s), (primal_h, primal),
        (frow_h, frow_s), (fcolv_h, fcol_v), (fcost_h, fcost),
    ]
    rest = [fetch(src, dst, in_sem.at[i + 2]) for i, (src, dst) in enumerate(inputs)]

    def at_offset(p):
        dx, dy, dz = p
        return (
            lax.rem(x + dx, XN) * 2 + core if dx else r,
            lax.rem(y + dy, YN) * ZN + lax.rem(z + dz + ZN, ZN),
        )

    sibling = (x * 2 + 1 - core, c)
    x_peers = [at_offset((d, 0, 0)) for d in X_PEERS]
    barrier = pltpu.get_barrier_semaphore()

    def greet(device):
        pl.semaphore_signal(barrier, inc=1, device_id=device, device_id_type=MESH)

    for p in PLANE_PEERS:
        greet(at_offset(p))
    for device in x_peers:
        greet(device)
    greet(sibling)

    xtile[...] = jnp.zeros_like(xtile)
    ytile[...] = jnp.zeros_like(ytile)

    for copy in first + rest:
        copy.wait()
    put_tiles(ytile, pairs(dual, ROWB))
    lane = lax.broadcasted_iota(jnp.int32, (1, LANES), 1)
    alive = lane < cnt_s[0]
    rows[...] = jnp.full((8, LANES), -1, jnp.int32)
    rows[0:1, 0:SLOTS] = bcol_v[...]
    rows[1:2, 0:SLOTS] = brow_v[...]
    rows[2:3, 0:NEW] = fcol_v[...]

    def twice(row, keep):
        kept = jnp.where(keep, row, -1).astype(F32)
        return jnp.where(lane < PAD, kept, pltpu.roll(kept, PAD, 1))

    my_cols = twice(rows[0:1, :], alive)
    my_rows = twice(rows[1:2, :], alive)
    new_cols = twice(rows[2:3, :], lane < NEW)
    row_ids = lax.broadcasted_iota(jnp.int32, (ROWB, LANES), 0).astype(F32)
    col_ids = lax.broadcasted_iota(jnp.int32, (COLB, LANES), 0).astype(F32)

    dem_sq = jnp.sum(demand[...] * demand[...], axis=0, keepdims=True)
    meta[...] = jnp.zeros_like(meta)
    meta[0:1, :] = my_cols
    meta[1:2, :] = dem_sq
    costrow[...] = jnp.sum(cost[...] * cost[...], axis=0, keepdims=True)
    price[...] = pairs(cost, COLB)
    xcur[...] = pairs(primal, COLB)

    def block_tile(ref, ids):
        tiles = ref.reshape(2, ref.shape[1] // 8, 8, LANES)

        def tile(s):
            at = ids[s]
            return jnp.concatenate([tiles[0, at], tiles[1, at]], axis=1).astype(BF)

        return tile

    my_chunk = lax.rem(y, 2) * 4 + lax.rem(z, 4)
    my_at = pl.multiple_of(my_chunk * CHUNK, CHUNK)
    tau = sigma = None
    fresh_copy = None
    for it in range(ITERS):
        for h in range(2):
            if it == 0:
                for copy in loads[h * LOADS // 2:(h + 1) * LOADS // 2]:
                    copy.wait()
            products(h * HALF, HALF, UNROLL, block_tile(ytile, brow_s), blk, prod8)
            half = pl.ds(h * HALF, HALF)
            prod[it, half, :] = summed(prod8, h * HALF, HALF)
            if it == 0 and h == 0:
                continue
            if it == 0:
                fresh_copy = fetch(fresh, frs, fresh_sem)
                pl.semaphore_wait(barrier, len(PLANE_PEERS) + len(X_PEERS) + 1)
                for d, device in enumerate(x_peers):
                    send(meta, metabuf.at[d], meta_send, meta_recv, device)
                half = pl.ds(0, SLOTS)
            for d, device in enumerate(x_peers):
                send(prod.at[it, half], pbuf.at[it, d, half], px_send.at[it], px_recv.at[it, d], device)
        if it == 0:
            for j, p in enumerate(PLANE_PEERS):
                send(costrow, costbuf.at[j], cost_send, cost_recv, at_offset(p))

            def turn(i, _):
                for u in range(UNROLL_T):
                    s = i * UNROLL_T + u
                    blk_t[s] = blk[s].T
                return 0

            lax.fori_loop(0, SLOTS // UNROLL_T, turn, 0)
        total = scatter(hot3(col_ids, my_cols), prod[it])
        if it == 0:
            wait_for(metabuf, meta_recv)
        for d in (1, 2, 0):
            wait_for(pbuf.at[it, d], px_recv.at[it, d])
            total = total + scatter(hot3(col_ids, metabuf[d, 0:1, :]), pbuf[it, d])
        dense[it] = total
        send(dense.at[it], sib.at[it], sib_send.at[it], sib_recv.at[it], sibling)
        if it == 0:
            dem4 = dem_sq + metabuf[0, 1:2, :] + metabuf[1, 1:2, :] + metabuf[2, 1:2, :]
            demrow[0] = dem4
            send(demrow.at[0], demrow.at[1], dem_send, dem_recv, sibling)
            wait_for(costbuf, cost_recv)
            cost_all = jnp.sum(costbuf[...], axis=0) + costrow[...]
            cost_total = jnp.sum(cost_all, axis=1, keepdims=True)
            wait_for(demrow.at[1], dem_recv)
            dem_total = jnp.sum(dem4 + demrow[1], axis=1, keepdims=True)
            omega = jnp.sqrt(cost_total) / jnp.sqrt(dem_total)
            tau = step_s[0] / omega
            sigma = step_s[0] * omega
        was = xcur[...]
        wait_for(sib.at[it], sib_recv.at[it])
        now = jnp.maximum(0.0, was - tau * (price[...] - (dense[it] + sib[it])))
        put_tiles(xtile, 2.0 * now - was)
        xcur[...] = now

        products(0, SLOTS, UNROLL, block_tile(xtile, bcol_s), blk_t, prod8)
        put_pairs(part.at[it], scatter(hot3(row_ids, my_rows), summed(prod8, 0, SLOTS)))
        for j, p in enumerate(PLANE_PEERS):
            target = at_offset(p)
            ty, tz = target[1] // ZN, lax.rem(target[1], ZN)
            at = pl.multiple_of((lax.rem(ty, 2) * 4 + lax.rem(tz, 4)) * CHUNK, CHUNK)
            send(part.at[it, pl.ds(at, CHUNK)], rsbuf.at[it, j], rs_send.at[it], rs_recv.at[it], target)
        if it == ITERS - 1:
            put_pairs(primal_o, xcur[...])
            put_primal = fetch(primal_o, primal_oh, out_sem.at[0])
        y_was = dual[pl.ds(my_at, CHUNK), :] if it == 0 else ybuf[it - 1, pl.ds(my_at, CHUNK), :]
        mine = part[it, pl.ds(my_at, CHUNK), :]
        wait_for(rsbuf.at[it], rs_recv.at[it])
        fore = mine + jnp.sum(rsbuf[it], axis=0)
        y_now = jnp.maximum(0.0, y_was + sigma * (demand[pl.ds(my_at, CHUNK), :] - fore))
        held = ybuf.at[it] if it < ITERS - 1 else yall.at[core, x]
        held[pl.ds(my_at, CHUNK), :] = y_now
        chunk = held.at[pl.ds(my_at, CHUNK)]
        for p in NEAR_PEERS if it < ITERS - 1 else LAST_PEERS:
            send(chunk, chunk, ag_send.at[it], ag_recv.at[it], at_offset(p))
        if it < ITERS - 1:
            wait_for(held.at[pl.ds(0, len(NEAR_PEERS) * CHUNK)], ag_recv.at[it])
            put_tiles(ytile, pairs(held, ROWB))

    new_hot = hot3(row_ids, new_cols)
    lane_row = lax.broadcasted_iota(jnp.int32, (8, EDGE), 0)
    fresh_copy.wait()
    wait_for(rsbuf.at[0], ag_recv.at[ITERS - 1])
    send(yall.at[core], yall.at[core], fs_send, fs_recv, sibling)
    dual_o[...] = yall[core, x]
    put_dual = fetch(dual_o, dual_oh, out_sem.at[1])
    wait_for(yall.at[core], fs_recv)

    yflat = yall.reshape(2 * XN * 2 * ROWB, LANES)

    def new_tile(s):
        block = frow_s[s]
        rr = block // ROWB
        at = lax.rem(rr, 2) * (XN * 2 * ROWB) + (rr // 2) * (2 * ROWB) + lax.rem(block, ROWB) * 2
        return piece_tile(yflat, at, lane_row)

    products(0, NEW, UNROLL_NEW, new_tile, frs, prod8)
    put_pairs(priced, scatter(new_hot, summed(prod8, 0, NEW)))
    reduced_o[...] = fcost[...] - priced[...]
    put_reduced = fetch(reduced_o, reduced_oh, out_sem.at[2])

    wait_for(yall.at[core], fs_send)
    wait_for(metabuf, meta_send)
    wait_for(costbuf, cost_send)
    wait_for(demrow.at[1], dem_send)
    for it in range(ITERS):
        wait_for(pbuf.at[it], px_send.at[it])
        wait_for(sib.at[it], sib_send.at[it])
        wait_for(rsbuf.at[it], rs_send.at[it])
        wait_for(rsbuf.at[it, pl.ds(0, len(NEAR_PEERS if it < ITERS - 1 else LAST_PEERS))], ag_send.at[it])
    put_primal.wait()
    put_dual.wait()
    put_reduced.wait()


def hand_over(*refs):
    sems = refs[-1]
    ins = [fetch(refs[i], refs[i + 6], sems.at[i]) for i in range(3)]
    outs = []
    for i in range(3):
        ins[i].wait()
        outs.append(fetch(refs[i + 6], refs[i + 3], sems.at[i + 3]))
    for copy in outs:
        copy.wait()


def local(
    blocks, block_row, block_col, block_count, primal, dual, cost, demand, step,
    fresh_pattern_blocks, fresh_block_row, fresh_block_column, fresh_pattern_cost,
):
    hbm = pl.BlockSpec(memory_space=pltpu.HBM)
    dma = pltpu.SemaphoreType.DMA
    smem_i = lambda n: pltpu.SMEM((n,), jnp.int32)
    vec_i = lambda n: pltpu.VMEM((1, n), jnp.int32)
    f32 = lambda *shape: pltpu.VMEM(shape, F32)
    rows2 = lambda v: v.reshape(-1, LANES)
    out_rows = (2 * COLB, 2 * ROWB, 2 * NEW)
    outs = pl.pallas_call(
        kernel,
        out_shape=tuple(jax.ShapeDtypeStruct((n, LANES), F32) for n in out_rows),
        in_specs=[hbm] * 15,
        out_specs=(hbm, hbm, hbm),
        scratch_shapes=[
            *[f32(n, LANES) for n in out_rows], dma((3,)),
            smem_i(SLOTS), smem_i(SLOTS), smem_i(1), smem_i(NEW), pltpu.SMEM((1,), F32),
            vec_i(SLOTS), vec_i(SLOTS), vec_i(NEW),
            f32(2 * COLB, LANES), f32(2 * ROWB, LANES), f32(2 * COLB, LANES), f32(2 * ROWB, LANES),
            f32(2 * NEW, LANES), pltpu.VMEM((8, LANES), jnp.int32),
            pltpu.VMEM((SLOTS, EDGE, EDGE), BF),
            pltpu.VMEM((SLOTS, EDGE, EDGE), BF),
            pltpu.VMEM((NEW, EDGE, EDGE), BF),
            f32(ITERS, SLOTS, EDGE), f32(ITERS, XN - 1, SLOTS, EDGE),
            f32(8, LANES), f32(XN - 1, 8, LANES),
            f32(ITERS, COLB, EDGE), f32(ITERS, COLB, EDGE),
            f32(2, 1, LANES), f32(1, LANES), f32(PLANE - 1, 1, LANES),
            f32(COLB, EDGE), f32(COLB, EDGE), f32(2, 8 * COLB, LANES), f32(2, 8 * ROWB, LANES),
            f32(2, 8 * SLOTS, LANES),
            f32(ITERS, 2 * ROWB, LANES), f32(ITERS, PLANE - 1, CHUNK, LANES),
            f32(ITERS, 2 * ROWB, LANES), f32(2, XN, 2 * ROWB, LANES),
            f32(2 * NEW, LANES),
            dma((13,)), dma((LOADS,)), dma,
            dma((ITERS,)), dma((ITERS, XN - 1)), dma, dma, dma, dma, dma, dma,
            dma((ITERS,)), dma((ITERS,)), dma((ITERS,)), dma((ITERS,)),
            dma((ITERS,)), dma((ITERS,)), dma, dma,
        ],
        compiler_params=pltpu.CompilerParams(
            collective_id=0, has_side_effects=True, vmem_limit_bytes=60 * 2**20
        ),
    )(
        block_row, block_col, block_count, fresh_block_row, step,
        block_col.reshape(1, -1), block_row.reshape(1, -1), fresh_block_column.reshape(1, -1),
        rows2(primal), rows2(dual), rows2(cost), rows2(demand), rows2(fresh_pattern_cost),
        blocks, fresh_pattern_blocks,
    )
    outs = pl.pallas_call(
        hand_over,
        out_shape=tuple(jax.ShapeDtypeStruct(o.shape, F32) for o in outs),
        in_specs=[hbm] * 3,
        out_specs=(hbm, hbm, hbm),
        scratch_shapes=[f32(n, LANES) for n in out_rows] + [dma((6,))],
        compiler_params=pltpu.CompilerParams(vmem_limit_bytes=60 * 2**20),
    )(*outs)
    return tuple(o.reshape(-1) for o in outs)


def solution(mesh):
    both = ("rows", "cols")
    placed = (
        P(both, None, None), P(both), P(both), P(both),
        P("cols"), P("rows"), P("cols"), P("rows"), P(),
        P(both, None, None), P(both), P(both), P(both),
    )
    return jax.shard_map(
        local, mesh=mesh, in_specs=placed,
        out_specs=(P("cols"), P("rows"), P(both)), check_vma=False,
    )
```

```python
import jax
import jax.numpy as jnp
from jax import lax
from jax.sharding import PartitionSpec as P
from jax.experimental import pallas as pl
from jax.experimental.pallas import tpu as pltpu

MESH = pl.DeviceIdType.MESH
ITERS = 2
EDGE = 256
LANES = 128
SLOTS = 48
HALF = SLOTS // 2
NEW = 32
XN, YN, ZN = 4, 4, 8
PLANE = YN * ZN
COLB = 128
ROWB = 32
CHUNK = 8
PAD = 64
BF = jnp.bfloat16
F32 = jnp.float32
LOADS = 4
UNROLL = 48
UNROLL_NEW = 32
UNROLL_T = 4


def hops(p):
    ring = lambda d, n: min(d % n, -d % n)
    return ring(p[0], XN) + ring(p[1], YN) + ring(p[2], ZN)


def far_first(peers):
    return sorted([p for p in peers if hops(p)], key=lambda p: -hops(p))


PLANE_PEERS = far_first([(0, dy, dz) for dy in range(YN) for dz in range(ZN)])
NEAR = [(0, dy, dz) for dy in (0, 1) for dz in (-1, 0, 1, 2)]
NEAR_PEERS = far_first(NEAR)
LAST_PEERS = far_first([(dx, dy, dz) for dx in range(XN) for _, dy, dz in NEAR])
X_PEERS = (2, 1, 3)


def split3(v):
    hi = v.astype(BF).astype(F32)
    rest = v - hi
    mid = rest.astype(BF).astype(F32)
    return hi, mid, rest - mid


def piece_tile(ref, at, lane_row):
    v = jnp.concatenate([ref[pl.ds(at, 1), :], ref[pl.ds(at + 1, 1), :]], axis=1)
    v = jnp.broadcast_to(v, (8, EDGE))
    hi, mid, lo = split3(v)
    tile = jnp.where(lane_row == 0, hi, jnp.where(lane_row == 1, mid, lo))
    return jnp.where(lane_row < 3, tile, 0.0).astype(BF)


def put_tiles(ref, val):
    n = val.shape[0]
    for k, part in enumerate(split3(val)):
        for h in range(2):
            ref[h, pl.ds(k, n, stride=8), :] = part[:, h * LANES:(h + 1) * LANES]


def pairs(ref, n):
    return jnp.concatenate([ref[pl.ds(0, n, stride=2), :], ref[pl.ds(1, n, stride=2), :]], axis=1)


def put_pairs(ref, val):
    n = val.shape[0]
    ref[pl.ds(0, n, stride=2), :] = val[:, :LANES]
    ref[pl.ds(1, n, stride=2), :] = val[:, LANES:]


def products(first, count, unroll, tile_of, blk_ref, out_ref):
    def step(i, _):
        for u in range(unroll):
            s = first + i * unroll + u
            res = jnp.dot(tile_of(s), blk_ref[s], preferred_element_type=F32)
            for h in range(2):
                out_ref[h, pl.ds(pl.multiple_of(s * 8, 8), 8), :] = res[:, h * LANES:(h + 1) * LANES]
        return 0

    if count == unroll:
        step(0, 0)
    else:
        lax.fori_loop(0, count // unroll, step, 0)


def summed(ref, first, count):
    def half(h):
        parts = [ref[h, pl.ds(first * 8 + k, count, stride=8), :] for k in range(3)]
        return parts[0] + parts[1] + parts[2]

    return jnp.concatenate([half(0), half(1)], axis=1)


def hot3(ids, row):
    lane = lax.broadcasted_iota(jnp.int32, (1, LANES), 1)
    third = jnp.where(lane < PAD, row, -1.0)
    n = ids.shape[0]
    hot = [(ids == jnp.broadcast_to(v, (n, LANES))).astype(F32).astype(BF) for v in (row, third)]
    return jnp.concatenate(hot, axis=1)


def scatter(hot, prod):
    n = prod.shape[0]
    zeros = jnp.zeros((PAD - n, EDGE), BF)
    rows = []
    for part in split3(prod):
        rows += [part.astype(BF), zeros]
    rows.append(jnp.zeros((PAD, EDGE), BF))
    return jnp.dot(hot, jnp.concatenate(rows, axis=0), preferred_element_type=F32)


def send(src, dst, send_sem, recv_sem, device):
    pltpu.make_async_remote_copy(
        src_ref=src, dst_ref=dst, send_sem=send_sem, recv_sem=recv_sem,
        device_id=device, device_id_type=MESH,
    ).start()


def wait_for(ref, sem):
    pltpu.make_async_copy(ref, ref, sem).wait()


def fetch(src, dst, sem):
    copy = pltpu.make_async_copy(src, dst, sem)
    copy.start()
    return copy


def kernel(
    brow_h, bcol_h, cnt_h, frow_h, step_h, bcolv_h, browv_h, fcolv_h,
    primal_h, dual_h, cost_h, demand_h, fcost_h, blocks, fresh,
    primal_oh, dual_oh, reduced_oh,
    primal_o, dual_o, reduced_o, out_sem,
    brow_s, bcol_s, cnt_s, frow_s, step_s, bcol_v, brow_v, fcol_v,
    primal, dual, cost, demand, fcost, rows,
    blk, blk_t, frs, prod, pbuf, meta, metabuf, dense, sib, demrow, costrow, costbuf,
    xcur, price, xtile, ytile, prod8, part, rsbuf, ybuf, yall, priced, hots, row_hot, new_hot,
    in_sem, load_sem, fresh_sem, px_send, px_recv, meta_send, meta_recv, cost_send, cost_recv,
    dem_send, dem_recv, sib_send, sib_recv, rs_send, rs_recv, ag_send, ag_recv, fs_send, fs_recv,
):
    r = lax.axis_index("rows")
    c = lax.axis_index("cols")
    x, core = r // 2, lax.rem(r, 2)
    y, z = c // ZN, lax.rem(c, ZN)
    per = SLOTS // LOADS

    def at_offset(p):
        dx, dy, dz = p
        return (
            lax.rem(x + dx, XN) * 2 + core if dx else r,
            lax.rem(y + dy, YN) * ZN + lax.rem(z + dz + ZN, ZN),
        )

    sibling = (x * 2 + 1 - core, c)
    x_peers = [at_offset((d, 0, 0)) for d in X_PEERS]
    barrier = pltpu.get_barrier_semaphore()

    def greet(device):
        pl.semaphore_signal(barrier, inc=1, device_id=device, device_id_type=MESH)

    plane = [at_offset(p) for p in PLANE_PEERS]
    for device in plane:
        greet(device)
    for device in x_peers:
        greet(device)
    greet(sibling)

    first = [
        fetch(src, dst, in_sem.at[i])
        for i, (src, dst) in enumerate([(brow_h, brow_s), (dual_h, dual)])
    ]
    loads = [
        fetch(blocks.at[pl.ds(i * per, per)], blk.at[pl.ds(i * per, per)], load_sem.at[i])
        for i in range(LOADS)
    ]
    inputs = [
        (cnt_h, cnt_s), (bcolv_h, bcol_v), (browv_h, brow_v), (cost_h, cost), (demand_h, demand),
        (step_h, step_s), (bcol_h, bcol_s), (primal_h, primal),
        (frow_h, frow_s), (fcolv_h, fcol_v), (fcost_h, fcost),
    ]
    rest = [fetch(src, dst, in_sem.at[i + 2]) for i, (src, dst) in enumerate(inputs)]

    xtile[...] = jnp.zeros_like(xtile)
    ytile[...] = jnp.zeros_like(ytile)

    for copy in first + rest:
        copy.wait()
    put_tiles(ytile, pairs(dual, ROWB))
    lane = lax.broadcasted_iota(jnp.int32, (1, LANES), 1)
    alive = lane < cnt_s[0]
    rows[...] = jnp.full((8, LANES), -1, jnp.int32)
    rows[0:1, 0:SLOTS] = bcol_v[...]
    rows[1:2, 0:SLOTS] = brow_v[...]
    rows[2:3, 0:NEW] = fcol_v[...]

    def twice(row, keep):
        kept = jnp.where(keep, row, -1).astype(F32)
        return jnp.where(lane < PAD, kept, pltpu.roll(kept, PAD, 1))

    my_cols = twice(rows[0:1, :], alive)
    my_rows = twice(rows[1:2, :], alive)
    new_cols = twice(rows[2:3, :], lane < NEW)
    row_ids = lax.broadcasted_iota(jnp.int32, (ROWB, LANES), 0).astype(F32)
    col_ids = lax.broadcasted_iota(jnp.int32, (COLB, LANES), 0).astype(F32)

    dem_sq = jnp.sum(demand[...] * demand[...], axis=0, keepdims=True)
    meta[...] = jnp.zeros_like(meta)
    meta[0:1, :] = my_cols
    meta[1:2, :] = dem_sq
    costrow[...] = jnp.sum(cost[...] * cost[...], axis=0, keepdims=True)
    price[...] = pairs(cost, COLB)
    xcur[...] = pairs(primal, COLB)

    def block_tile(ref, ids):
        tiles = ref.reshape(2, ref.shape[1] // 8, 8, LANES)

        def tile(s):
            at = ids[s]
            return jnp.concatenate([tiles[0, at], tiles[1, at]], axis=1).astype(BF)

        return tile

    my_chunk = lax.rem(y, 2) * 4 + lax.rem(z, 4)
    my_at = pl.multiple_of(my_chunk * CHUNK, CHUNK)
    chunk_at = [
        pl.multiple_of((lax.rem(y + dy, 2) * 4 + lax.rem(z + dz, 4)) * CHUNK, CHUNK)
        for _, dy, dz in PLANE_PEERS
    ]
    near = [at_offset(p) for p in NEAR_PEERS]
    last = [at_offset(p) for p in LAST_PEERS]
    pending = []
    left = lambda ref, sem: pending.append(lambda: wait_for(ref, sem))
    tau = sigma = None
    fresh_copy = None
    for it in range(ITERS):
        for h in range(2):
            if it == 0:
                for copy in loads[h * LOADS // 2:(h + 1) * LOADS // 2]:
                    copy.wait()
            products(h * HALF, HALF, HALF, block_tile(ytile, brow_s), blk, prod8)
            half = pl.ds(h * HALF, HALF)
            prod[it, half, :] = summed(prod8, h * HALF, HALF)
            if it == 0 and h == 0:
                continue
            if it == 0:
                fresh_copy = fetch(fresh, frs, fresh_sem)
                pl.semaphore_wait(barrier, len(PLANE_PEERS) + len(X_PEERS) + 1)
                for d, device in enumerate(x_peers):
                    send(meta, metabuf.at[d], meta_send, meta_recv, device)
                left(metabuf, meta_send)
                half = pl.ds(0, SLOTS)
            for d, device in enumerate(x_peers):
                send(prod.at[it, half], pbuf.at[it, d, half], px_send.at[it], px_recv.at[it, d], device)
        left(pbuf.at[it], px_send.at[it])
        if it == 0:
            for j, device in enumerate(plane):
                send(costrow, costbuf.at[j], cost_send, cost_recv, device)
            left(costbuf, cost_send)

            def turn(i, _):
                for u in range(UNROLL_T):
                    s = i * UNROLL_T + u
                    blk_t[s] = blk[s].T
                return 0

            lax.fori_loop(0, SLOTS // UNROLL_T, turn, 0)
        if it == 0:
            hots[XN - 1] = hot3(col_ids, my_cols)
            wait_for(metabuf, meta_recv)
            for d in range(XN - 1):
                hots[d] = hot3(col_ids, metabuf[d, 0:1, :])
            row_hot[...] = hot3(row_ids, my_rows)
            new_hot[...] = hot3(row_ids, new_cols)
        total = scatter(hots[XN - 1], prod[it])
        for d in (1, 2, 0):
            wait_for(pbuf.at[it, d], px_recv.at[it, d])
            total = total + scatter(hots[d], pbuf[it, d])
        dense[it] = total
        send(dense.at[it], sib.at[it], sib_send.at[it], sib_recv.at[it], sibling)
        left(sib.at[it], sib_send.at[it])
        if it == 0:
            dem4 = dem_sq + metabuf[0, 1:2, :] + metabuf[1, 1:2, :] + metabuf[2, 1:2, :]
            demrow[0] = dem4
            send(demrow.at[0], demrow.at[1], dem_send, dem_recv, sibling)
            left(demrow.at[1], dem_send)
            wait_for(costbuf, cost_recv)
            cost_all = jnp.sum(costbuf[...], axis=0) + costrow[...]
            cost_total = jnp.sum(cost_all, axis=1, keepdims=True)
            wait_for(demrow.at[1], dem_recv)
            dem_total = jnp.sum(dem4 + demrow[1], axis=1, keepdims=True)
            omega = jnp.sqrt(cost_total) / jnp.sqrt(dem_total)
            tau = step_s[0] / omega
            sigma = step_s[0] * omega
        was = xcur[...]
        wait_for(sib.at[it], sib_recv.at[it])
        now = jnp.maximum(0.0, was - tau * (price[...] - (dense[it] + sib[it])))
        put_tiles(xtile, 2.0 * now - was)
        xcur[...] = now

        products(0, SLOTS, UNROLL, block_tile(xtile, bcol_s), blk_t, prod8)
        put_pairs(part.at[it], scatter(row_hot[...], summed(prod8, 0, SLOTS)))
        for j, device in enumerate(plane):
            send(part.at[it, pl.ds(chunk_at[j], CHUNK)], rsbuf.at[it, j], rs_send.at[it], rs_recv.at[it], device)
        left(rsbuf.at[it], rs_send.at[it])
        if it == ITERS - 1:
            put_pairs(primal_o, xcur[...])
            pending.append(fetch(primal_o, primal_oh, out_sem.at[0]).wait)
        y_was = dual[pl.ds(my_at, CHUNK), :] if it == 0 else ybuf[it - 1, pl.ds(my_at, CHUNK), :]
        mine = part[it, pl.ds(my_at, CHUNK), :]
        wait_for(rsbuf.at[it], rs_recv.at[it])
        fore = mine + jnp.sum(rsbuf[it], axis=0)
        y_now = jnp.maximum(0.0, y_was + sigma * (demand[pl.ds(my_at, CHUNK), :] - fore))
        held = ybuf.at[it] if it < ITERS - 1 else yall.at[core, x]
        held[pl.ds(my_at, CHUNK), :] = y_now
        chunk = held.at[pl.ds(my_at, CHUNK)]
        peers = near if it < ITERS - 1 else last
        for device in peers:
            send(chunk, chunk, ag_send.at[it], ag_recv.at[it], device)
        left(rsbuf.at[it, pl.ds(0, len(peers))], ag_send.at[it])
        if it < ITERS - 1:
            wait_for(held.at[pl.ds(0, len(NEAR_PEERS) * CHUNK)], ag_recv.at[it])
            put_tiles(ytile, pairs(held, ROWB))

    lane_row = lax.broadcasted_iota(jnp.int32, (8, EDGE), 0)
    fresh_copy.wait()
    wait_for(rsbuf.at[0], ag_recv.at[ITERS - 1])
    send(yall.at[core], yall.at[core], fs_send, fs_recv, sibling)
    left(yall.at[core], fs_send)
    dual_o[...] = yall[core, x]
    pending.append(fetch(dual_o, dual_oh, out_sem.at[1]).wait)
    wait_for(yall.at[core], fs_recv)

    yflat = yall.reshape(2 * XN * 2 * ROWB, LANES)

    def new_tile(s):
        block = frow_s[s]
        rr = block // ROWB
        at = lax.rem(rr, 2) * (XN * 2 * ROWB) + (rr // 2) * (2 * ROWB) + lax.rem(block, ROWB) * 2
        return piece_tile(yflat, at, lane_row)

    products(0, NEW, UNROLL_NEW, new_tile, frs, prod8)
    put_pairs(priced, scatter(new_hot[...], summed(prod8, 0, NEW)))
    reduced_o[...] = fcost[...] - priced[...]
    pending.append(fetch(reduced_o, reduced_oh, out_sem.at[2]).wait)

    for done in pending:
        done()


def hand_over(*refs):
    sems = refs[-1]
    ins = [fetch(refs[i], refs[i + 6], sems.at[i]) for i in range(3)]
    outs = []
    for i in range(3):
        ins[i].wait()
        outs.append(fetch(refs[i + 6], refs[i + 3], sems.at[i + 3]))
    for copy in outs:
        copy.wait()


def local(
    blocks, block_row, block_col, block_count, primal, dual, cost, demand, step,
    fresh_pattern_blocks, fresh_block_row, fresh_block_column, fresh_pattern_cost,
):
    hbm = pl.BlockSpec(memory_space=pltpu.HBM)
    dma = pltpu.SemaphoreType.DMA
    smem_i = lambda n: pltpu.SMEM((n,), jnp.int32)
    vec_i = lambda n: pltpu.VMEM((1, n), jnp.int32)
    f32 = lambda *shape: pltpu.VMEM(shape, F32)
    rows2 = lambda v: v.reshape(-1, LANES)
    out_rows = (2 * COLB, 2 * ROWB, 2 * NEW)
    outs = pl.pallas_call(
        kernel,
        out_shape=tuple(jax.ShapeDtypeStruct((n, LANES), F32) for n in out_rows),
        in_specs=[hbm] * 15,
        out_specs=(hbm, hbm, hbm),
        scratch_shapes=[
            *[f32(n, LANES) for n in out_rows], dma((3,)),
            smem_i(SLOTS), smem_i(SLOTS), smem_i(1), smem_i(NEW), pltpu.SMEM((1,), F32),
            vec_i(SLOTS), vec_i(SLOTS), vec_i(NEW),
            f32(2 * COLB, LANES), f32(2 * ROWB, LANES), f32(2 * COLB, LANES), f32(2 * ROWB, LANES),
            f32(2 * NEW, LANES), pltpu.VMEM((8, LANES), jnp.int32),
            pltpu.VMEM((SLOTS, EDGE, EDGE), BF),
            pltpu.VMEM((SLOTS, EDGE, EDGE), BF),
            pltpu.VMEM((NEW, EDGE, EDGE), BF),
            f32(ITERS, SLOTS, EDGE), f32(ITERS, XN - 1, SLOTS, EDGE),
            f32(8, LANES), f32(XN - 1, 8, LANES),
            f32(ITERS, COLB, EDGE), f32(ITERS, COLB, EDGE),
            f32(2, 1, LANES), f32(1, LANES), f32(PLANE - 1, 1, LANES),
            f32(COLB, EDGE), f32(COLB, EDGE), f32(2, 8 * COLB, LANES), f32(2, 8 * ROWB, LANES),
            f32(2, 8 * SLOTS, LANES),
            f32(ITERS, 2 * ROWB, LANES), f32(ITERS, PLANE - 1, CHUNK, LANES),
            f32(ITERS, 2 * ROWB, LANES), f32(2, XN, 2 * ROWB, LANES),
            f32(2 * NEW, LANES), pltpu.VMEM((XN, COLB, EDGE), BF),
            pltpu.VMEM((ROWB, EDGE), BF), pltpu.VMEM((NEW, EDGE), BF),
            dma((13,)), dma((LOADS,)), dma,
            dma((ITERS,)), dma((ITERS, XN - 1)), dma, dma, dma, dma, dma, dma,
            dma((ITERS,)), dma((ITERS,)), dma((ITERS,)), dma((ITERS,)),
            dma((ITERS,)), dma((ITERS,)), dma, dma,
        ],
        compiler_params=pltpu.CompilerParams(
            collective_id=0, has_side_effects=True, vmem_limit_bytes=60 * 2**20
        ),
    )(
        block_row, block_col, block_count, fresh_block_row, step,
        block_col.reshape(1, -1), block_row.reshape(1, -1), fresh_block_column.reshape(1, -1),
        rows2(primal), rows2(dual), rows2(cost), rows2(demand), rows2(fresh_pattern_cost),
        blocks, fresh_pattern_blocks,
    )
    outs = pl.pallas_call(
        hand_over,
        out_shape=tuple(jax.ShapeDtypeStruct(o.shape, F32) for o in outs),
        in_specs=[hbm] * 3,
        out_specs=(hbm, hbm, hbm),
        scratch_shapes=[f32(n, LANES) for n in out_rows] + [dma((6,))],
        compiler_params=pltpu.CompilerParams(vmem_limit_bytes=60 * 2**20),
    )(*outs)
    return tuple(o.reshape(-1) for o in outs)


def solution(mesh):
    both = ("rows", "cols")
    placed = (
        P(both, None, None), P(both), P(both), P(both),
        P("cols"), P("rows"), P("cols"), P("rows"), P(),
        P(both, None, None), P(both), P(both), P(both),
    )
    return jax.shard_map(
        local, mesh=mesh, in_specs=placed,
        out_specs=(P("cols"), P("rows"), P(both)), check_vma=False,
    )
```

```python
import jax
import jax.numpy as jnp
from jax import lax
from jax.sharding import PartitionSpec as P
from jax.experimental import pallas as pl
from jax.experimental.pallas import tpu as pltpu

MESH = pl.DeviceIdType.MESH
ITERS = 2
EDGE = 256
LANES = 128
SLOTS = 48
THIRD = SLOTS // 3
NEW = 32
XN, YN, ZN = 4, 4, 8
PLANE = YN * ZN
COLB = 128
ROWB = 32
CHUNK = 8
PAD = 64
BF = jnp.bfloat16
F32 = jnp.float32
LOADS = 3
UNROLL = 48
UNROLL_NEW = 32
UNROLL_T = 4


def hops(p):
    ring = lambda d, n: min(d % n, -d % n)
    return ring(p[0], XN) + ring(p[1], YN) + ring(p[2], ZN)


def far_first(peers):
    return sorted([p for p in peers if hops(p)], key=lambda p: -hops(p))


PLANE_PEERS = far_first([(0, dy, dz) for dy in range(YN) for dz in range(ZN)])
NEAR = [(0, dy, dz) for dy in (0, 1) for dz in (-1, 0, 1, 2)]
NEAR_PEERS = far_first(NEAR)
LAST_PEERS = far_first([(dx, dy, dz) for dx in range(XN) for _, dy, dz in NEAR])
X_PEERS = (2, 1, 3)


def split3(v):
    hi = v.astype(BF).astype(F32)
    rest = v - hi
    mid = rest.astype(BF).astype(F32)
    return hi, mid, rest - mid


def piece_tile(ref, at, lane_row):
    v = jnp.concatenate([ref[pl.ds(at, 1), :], ref[pl.ds(at + 1, 1), :]], axis=1)
    v = jnp.broadcast_to(v, (8, EDGE))
    hi, mid, lo = split3(v)
    tile = jnp.where(lane_row == 0, hi, jnp.where(lane_row == 1, mid, lo))
    return jnp.where(lane_row < 3, tile, 0.0).astype(BF)


def put_tiles(ref, val):
    n = val.shape[0]
    for k, part in enumerate(split3(val)):
        for h in range(2):
            ref[h, pl.ds(k, n, stride=8), :] = part[:, h * LANES:(h + 1) * LANES]


def pairs(ref, n):
    return jnp.concatenate([ref[pl.ds(0, n, stride=2), :], ref[pl.ds(1, n, stride=2), :]], axis=1)


def put_pairs(ref, val):
    n = val.shape[0]
    ref[pl.ds(0, n, stride=2), :] = val[:, :LANES]
    ref[pl.ds(1, n, stride=2), :] = val[:, LANES:]


def products(first, count, unroll, tile_of, blk_ref, out_ref):
    def step(i, _):
        for u in range(unroll):
            s = first + i * unroll + u
            res = jnp.dot(tile_of(s), blk_ref[s], preferred_element_type=F32)
            for h in range(2):
                out_ref[h, pl.ds(pl.multiple_of(s * 8, 8), 8), :] = res[:, h * LANES:(h + 1) * LANES]
        return 0

    if count == unroll:
        step(0, 0)
    else:
        lax.fori_loop(0, count // unroll, step, 0)


def summed(ref, first, count):
    def half(h):
        parts = [ref[h, pl.ds(first * 8 + k, count, stride=8), :] for k in range(3)]
        return parts[0] + parts[1] + parts[2]

    return jnp.concatenate([half(0), half(1)], axis=1)


def hot3(ids, row):
    lane = lax.broadcasted_iota(jnp.int32, (1, LANES), 1)
    third = jnp.where(lane < PAD, row, -1.0)
    n = ids.shape[0]
    hot = [(ids == jnp.broadcast_to(v, (n, LANES))).astype(F32).astype(BF) for v in (row, third)]
    return jnp.concatenate(hot, axis=1)


def scatter(hot, prod):
    n = prod.shape[0]
    zeros = jnp.zeros((PAD - n, EDGE), BF)
    rows = []
    for part in split3(prod):
        rows += [part.astype(BF), zeros]
    rows.append(jnp.zeros((PAD, EDGE), BF))
    return jnp.dot(hot, jnp.concatenate(rows, axis=0), preferred_element_type=F32)


def send(src, dst, send_sem, recv_sem, device):
    pltpu.make_async_remote_copy(
        src_ref=src, dst_ref=dst, send_sem=send_sem, recv_sem=recv_sem,
        device_id=device, device_id_type=MESH,
    ).start()


def wait_for(ref, sem):
    pltpu.make_async_copy(ref, ref, sem).wait()


def fetch(src, dst, sem):
    copy = pltpu.make_async_copy(src, dst, sem)
    copy.start()
    return copy


def kernel(
    brow_h, bcol_h, cnt_h, frow_h, step_h, bcolv_h, browv_h, fcolv_h,
    primal_h, dual_h, cost_h, demand_h, fcost_h, blocks, fresh,
    primal_oh, dual_oh, reduced_oh,
    primal_o, dual_o, reduced_o, out_sem,
    brow_s, bcol_s, cnt_s, frow_s, step_s, bcol_v, brow_v, fcol_v,
    primal, dual, cost, demand, fcost, rows,
    blk, blk_t, frs, prod, pbuf, meta, metabuf, dense, sib, demrow, costrow, costbuf,
    xcur, price, xtile, ytile, prod8, part, rsbuf, ybuf, yall, priced, hots, row_hot, new_hot,
    in_sem, load_sem, fresh_sem, px_send, px_recv, meta_send, meta_recv, cost_send, cost_recv,
    dem_send, dem_recv, sib_send, sib_recv, rs_send, rs_recv, ag_send, ag_recv, fs_send, fs_recv,
):
    r = lax.axis_index("rows")
    c = lax.axis_index("cols")
    x, core = r // 2, lax.rem(r, 2)
    y, z = c // ZN, lax.rem(c, ZN)
    per = SLOTS // LOADS

    def at_offset(p):
        dx, dy, dz = p
        return (
            lax.rem(x + dx, XN) * 2 + core if dx else r,
            lax.rem(y + dy, YN) * ZN + lax.rem(z + dz + ZN, ZN),
        )

    sibling = (x * 2 + 1 - core, c)
    x_peers = [at_offset((d, 0, 0)) for d in X_PEERS]
    barrier = pltpu.get_barrier_semaphore()

    def greet(device):
        pl.semaphore_signal(barrier, inc=1, device_id=device, device_id_type=MESH)

    plane = [at_offset(p) for p in PLANE_PEERS]
    for device in plane:
        greet(device)
    for device in x_peers:
        greet(device)
    greet(sibling)

    first = [
        fetch(src, dst, in_sem.at[i])
        for i, (src, dst) in enumerate([(brow_h, brow_s), (dual_h, dual)])
    ]
    loads = [
        fetch(blocks.at[pl.ds(i * per, per)], blk.at[pl.ds(i * per, per)], load_sem.at[i])
        for i in range(LOADS)
    ]
    inputs = [
        (cnt_h, cnt_s), (bcolv_h, bcol_v), (browv_h, brow_v), (cost_h, cost), (demand_h, demand),
        (step_h, step_s), (bcol_h, bcol_s), (primal_h, primal),
        (frow_h, frow_s), (fcolv_h, fcol_v), (fcost_h, fcost),
    ]
    rest = [fetch(src, dst, in_sem.at[i + 2]) for i, (src, dst) in enumerate(inputs)]

    xtile[...] = jnp.zeros_like(xtile)
    ytile[...] = jnp.zeros_like(ytile)

    for copy in first + rest:
        copy.wait()
    put_tiles(ytile, pairs(dual, ROWB))
    lane = lax.broadcasted_iota(jnp.int32, (1, LANES), 1)
    alive = lane < cnt_s[0]
    rows[...] = jnp.full((8, LANES), -1, jnp.int32)
    rows[0:1, 0:SLOTS] = bcol_v[...]
    rows[1:2, 0:SLOTS] = brow_v[...]
    rows[2:3, 0:NEW] = fcol_v[...]

    def twice(row, keep):
        kept = jnp.where(keep, row, -1).astype(F32)
        return jnp.where(lane < PAD, kept, pltpu.roll(kept, PAD, 1))

    my_cols = twice(rows[0:1, :], alive)
    my_rows = twice(rows[1:2, :], alive)
    new_cols = twice(rows[2:3, :], lane < NEW)
    row_ids = lax.broadcasted_iota(jnp.int32, (ROWB, LANES), 0).astype(F32)
    col_ids = lax.broadcasted_iota(jnp.int32, (COLB, LANES), 0).astype(F32)

    dem_sq = jnp.sum(demand[...] * demand[...], axis=0, keepdims=True)
    meta[...] = jnp.zeros_like(meta)
    meta[0:1, :] = my_cols
    meta[1:2, :] = dem_sq
    costrow[...] = jnp.sum(cost[...] * cost[...], axis=0, keepdims=True)
    price[...] = pairs(cost, COLB)
    xcur[...] = pairs(primal, COLB)

    def block_tile(ref, ids):
        tiles = ref.reshape(2, ref.shape[1] // 8, 8, LANES)

        def tile(s):
            at = ids[s]
            return jnp.concatenate([tiles[0, at], tiles[1, at]], axis=1).astype(BF)

        return tile

    my_chunk = lax.rem(y, 2) * 4 + lax.rem(z, 4)
    my_at = pl.multiple_of(my_chunk * CHUNK, CHUNK)
    chunk_at = [
        pl.multiple_of((lax.rem(y + dy, 2) * 4 + lax.rem(z + dz, 4)) * CHUNK, CHUNK)
        for _, dy, dz in PLANE_PEERS
    ]
    near = [at_offset(p) for p in NEAR_PEERS]
    last = [at_offset(p) for p in LAST_PEERS]
    pending = []
    left = lambda ref, sem: pending.append(lambda: wait_for(ref, sem))
    tau = sigma = None
    fresh_copy = None
    for it in range(ITERS):
        for h in range(LOADS):
            if it == 0:
                for copy in loads[h:h + 1]:
                    copy.wait()
            products(h * THIRD, THIRD, THIRD, block_tile(ytile, brow_s), blk, prod8)
            half = pl.ds(h * THIRD, THIRD)
            prod[it, half, :] = summed(prod8, h * THIRD, THIRD)
            if it == 0 and h < LOADS - 1:
                continue
            if it == 0:
                fresh_copy = fetch(fresh, frs, fresh_sem)
                pl.semaphore_wait(barrier, len(PLANE_PEERS) + len(X_PEERS) + 1)
                for d, device in enumerate(x_peers):
                    send(meta, metabuf.at[d], meta_send, meta_recv, device)
                left(metabuf, meta_send)
                half = pl.ds(0, SLOTS)
            for d, device in enumerate(x_peers):
                send(prod.at[it, half], pbuf.at[it, d, half], px_send.at[it], px_recv.at[it, d], device)
        left(pbuf.at[it], px_send.at[it])
        if it == 0:
            for j, device in enumerate(plane):
                send(costrow, costbuf.at[j], cost_send, cost_recv, device)
            left(costbuf, cost_send)

            def turn(i, _):
                for u in range(UNROLL_T):
                    s = i * UNROLL_T + u
                    blk_t[s] = blk[s].T
                return 0

            lax.fori_loop(0, SLOTS // UNROLL_T, turn, 0)
        if it == 0:
            hots[XN - 1] = hot3(col_ids, my_cols)
            wait_for(metabuf, meta_recv)
            for d in range(XN - 1):
                hots[d] = hot3(col_ids, metabuf[d, 0:1, :])
            row_hot[...] = hot3(row_ids, my_rows)
            new_hot[...] = hot3(row_ids, new_cols)
        total = scatter(hots[XN - 1], prod[it])
        for d in (1, 2, 0):
            wait_for(pbuf.at[it, d], px_recv.at[it, d])
            total = total + scatter(hots[d], pbuf[it, d])
        dense[it] = total
        send(dense.at[it], sib.at[it], sib_send.at[it], sib_recv.at[it], sibling)
        left(sib.at[it], sib_send.at[it])
        if it == 0:
            dem4 = dem_sq + metabuf[0, 1:2, :] + metabuf[1, 1:2, :] + metabuf[2, 1:2, :]
            demrow[0] = dem4
            send(demrow.at[0], demrow.at[1], dem_send, dem_recv, sibling)
            left(demrow.at[1], dem_send)
            wait_for(costbuf, cost_recv)
            cost_all = jnp.sum(costbuf[...], axis=0) + costrow[...]
            cost_total = jnp.sum(cost_all, axis=1, keepdims=True)
            wait_for(demrow.at[1], dem_recv)
            dem_total = jnp.sum(dem4 + demrow[1], axis=1, keepdims=True)
            omega = jnp.sqrt(cost_total) / jnp.sqrt(dem_total)
            tau = step_s[0] / omega
            sigma = step_s[0] * omega
        was = xcur[...]
        wait_for(sib.at[it], sib_recv.at[it])
        now = jnp.maximum(0.0, was - tau * (price[...] - (dense[it] + sib[it])))
        put_tiles(xtile, 2.0 * now - was)
        xcur[...] = now

        products(0, SLOTS, UNROLL, block_tile(xtile, bcol_s), blk_t, prod8)
        put_pairs(part.at[it], scatter(row_hot[...], summed(prod8, 0, SLOTS)))
        for j, device in enumerate(plane):
            send(part.at[it, pl.ds(chunk_at[j], CHUNK)], rsbuf.at[it, j], rs_send.at[it], rs_recv.at[it], device)
        left(rsbuf.at[it], rs_send.at[it])
        if it == ITERS - 1:
            put_pairs(primal_o, xcur[...])
            pending.append(fetch(primal_o, primal_oh, out_sem.at[0]).wait)
        y_was = dual[pl.ds(my_at, CHUNK), :] if it == 0 else ybuf[it - 1, pl.ds(my_at, CHUNK), :]
        mine = part[it, pl.ds(my_at, CHUNK), :]
        wait_for(rsbuf.at[it], rs_recv.at[it])
        fore = mine + jnp.sum(rsbuf[it], axis=0)
        y_now = jnp.maximum(0.0, y_was + sigma * (demand[pl.ds(my_at, CHUNK), :] - fore))
        held = ybuf.at[it] if it < ITERS - 1 else yall.at[core, x]
        held[pl.ds(my_at, CHUNK), :] = y_now
        chunk = held.at[pl.ds(my_at, CHUNK)]
        peers = near if it < ITERS - 1 else last
        for device in peers:
            send(chunk, chunk, ag_send.at[it], ag_recv.at[it], device)
        left(rsbuf.at[it, pl.ds(0, len(peers))], ag_send.at[it])
        if it < ITERS - 1:
            wait_for(held.at[pl.ds(0, len(NEAR_PEERS) * CHUNK)], ag_recv.at[it])
            put_tiles(ytile, pairs(held, ROWB))

    lane_row = lax.broadcasted_iota(jnp.int32, (8, EDGE), 0)
    fresh_copy.wait()
    wait_for(rsbuf.at[0], ag_recv.at[ITERS - 1])
    send(yall.at[core], yall.at[core], fs_send, fs_recv, sibling)
    left(yall.at[core], fs_send)
    dual_o[...] = yall[core, x]
    pending.append(fetch(dual_o, dual_oh, out_sem.at[1]).wait)
    wait_for(yall.at[core], fs_recv)

    yflat = yall.reshape(2 * XN * 2 * ROWB, LANES)

    def new_tile(s):
        block = frow_s[s]
        rr = block // ROWB
        at = lax.rem(rr, 2) * (XN * 2 * ROWB) + (rr // 2) * (2 * ROWB) + lax.rem(block, ROWB) * 2
        return piece_tile(yflat, at, lane_row)

    products(0, NEW, UNROLL_NEW, new_tile, frs, prod8)
    put_pairs(priced, scatter(new_hot[...], summed(prod8, 0, NEW)))
    reduced_o[...] = fcost[...] - priced[...]
    pending.append(fetch(reduced_o, reduced_oh, out_sem.at[2]).wait)

    for done in pending:
        done()


def hand_over(*refs):
    sems = refs[-1]
    ins = [fetch(refs[i], refs[i + 6], sems.at[i]) for i in range(3)]
    outs = []
    for i in range(3):
        ins[i].wait()
        outs.append(fetch(refs[i + 6], refs[i + 3], sems.at[i + 3]))
    for copy in outs:
        copy.wait()


def local(
    blocks, block_row, block_col, block_count, primal, dual, cost, demand, step,
    fresh_pattern_blocks, fresh_block_row, fresh_block_column, fresh_pattern_cost,
):
    hbm = pl.BlockSpec(memory_space=pltpu.HBM)
    dma = pltpu.SemaphoreType.DMA
    smem_i = lambda n: pltpu.SMEM((n,), jnp.int32)
    vec_i = lambda n: pltpu.VMEM((1, n), jnp.int32)
    f32 = lambda *shape: pltpu.VMEM(shape, F32)
    rows2 = lambda v: v.reshape(-1, LANES)
    out_rows = (2 * COLB, 2 * ROWB, 2 * NEW)
    outs = pl.pallas_call(
        kernel,
        out_shape=tuple(jax.ShapeDtypeStruct((n, LANES), F32) for n in out_rows),
        in_specs=[hbm] * 15,
        out_specs=(hbm, hbm, hbm),
        scratch_shapes=[
            *[f32(n, LANES) for n in out_rows], dma((3,)),
            smem_i(SLOTS), smem_i(SLOTS), smem_i(1), smem_i(NEW), pltpu.SMEM((1,), F32),
            vec_i(SLOTS), vec_i(SLOTS), vec_i(NEW),
            f32(2 * COLB, LANES), f32(2 * ROWB, LANES), f32(2 * COLB, LANES), f32(2 * ROWB, LANES),
            f32(2 * NEW, LANES), pltpu.VMEM((8, LANES), jnp.int32),
            pltpu.VMEM((SLOTS, EDGE, EDGE), BF),
            pltpu.VMEM((SLOTS, EDGE, EDGE), BF),
            pltpu.VMEM((NEW, EDGE, EDGE), BF),
            f32(ITERS, SLOTS, EDGE), f32(ITERS, XN - 1, SLOTS, EDGE),
            f32(8, LANES), f32(XN - 1, 8, LANES),
            f32(ITERS, COLB, EDGE), f32(ITERS, COLB, EDGE),
            f32(2, 1, LANES), f32(1, LANES), f32(PLANE - 1, 1, LANES),
            f32(COLB, EDGE), f32(COLB, EDGE), f32(2, 8 * COLB, LANES), f32(2, 8 * ROWB, LANES),
            f32(2, 8 * SLOTS, LANES),
            f32(ITERS, 2 * ROWB, LANES), f32(ITERS, PLANE - 1, CHUNK, LANES),
            f32(ITERS, 2 * ROWB, LANES), f32(2, XN, 2 * ROWB, LANES),
            f32(2 * NEW, LANES), pltpu.VMEM((XN, COLB, EDGE), BF),
            pltpu.VMEM((ROWB, EDGE), BF), pltpu.VMEM((NEW, EDGE), BF),
            dma((13,)), dma((LOADS,)), dma,
            dma((ITERS,)), dma((ITERS, XN - 1)), dma, dma, dma, dma, dma, dma,
            dma((ITERS,)), dma((ITERS,)), dma((ITERS,)), dma((ITERS,)),
            dma((ITERS,)), dma((ITERS,)), dma, dma,
        ],
        compiler_params=pltpu.CompilerParams(
            collective_id=0, has_side_effects=True, vmem_limit_bytes=60 * 2**20
        ),
    )(
        block_row, block_col, block_count, fresh_block_row, step,
        block_col.reshape(1, -1), block_row.reshape(1, -1), fresh_block_column.reshape(1, -1),
        rows2(primal), rows2(dual), rows2(cost), rows2(demand), rows2(fresh_pattern_cost),
        blocks, fresh_pattern_blocks,
    )
    outs = pl.pallas_call(
        hand_over,
        out_shape=tuple(jax.ShapeDtypeStruct(o.shape, F32) for o in outs),
        in_specs=[hbm] * 3,
        out_specs=(hbm, hbm, hbm),
        scratch_shapes=[f32(n, LANES) for n in out_rows] + [dma((6,))],
        compiler_params=pltpu.CompilerParams(vmem_limit_bytes=60 * 2**20),
    )(*outs)
    return tuple(o.reshape(-1) for o in outs)


def solution(mesh):
    both = ("rows", "cols")
    placed = (
        P(both, None, None), P(both), P(both), P(both),
        P("cols"), P("rows"), P("cols"), P("rows"), P(),
        P(both, None, None), P(both), P(both), P(both),
    )
    return jax.shard_map(
        local, mesh=mesh, in_specs=placed,
        out_specs=(P("cols"), P("rows"), P(both)), check_vma=False,
    )
```
